32 devices in a mesh: irrep: 4 (over z), row: 8 (over y, x, core).
Axes of the slice: x: 2, y: 2, z: 4, core: 2. Of those that a mesh axis runs over, the one named last changes fastest.
Arguments:
- densities: float32 [4, 2048, 512], P('irrep', 'row'), may hold values from -6 to 6
- reduced_kernel: float32 [4, 12288, 2048], P('irrep', 'row'), may hold values from -0.125 to 0.125
Outputs:
- potentials: float32 [4, 12288, 512], P('irrep', 'row')
The draws below stay inside these ranges and needn't reach their ends.
All inputs are finite; a program needn't handle non-finite values.
Results may differ from the reference program's by a relative error of at most 0.000086.
Values sent between devices are 32-bit elements; how exact they have to be, the bound alone decides.
No kernel may reach another device: no remote copies, remote signals or barrier semaphores. Data moves between devices by JAX's collectives and lax.ppermute only.
A program may use at most 128 MiB of HBM per device.

```python
import math
import jax
import jax.numpy as jnp
from jax import lax

EXCITE = 512
TARGETS = 12288
SOURCES = 2048
N_IRREP = 4


def level_of(rng, dims, shards, least, top_value):
    loudness, own = 1.0, jax.random.fold_in(rng, 6)
    for axis_at, shards_of in shards:
        heights = jnp.exp(jax.random.uniform(jax.random.fold_in(own, axis_at), (shards_of,), jnp.float32, least / len(shards), top_value / len(shards)))
        loudness = loudness * jnp.repeat(heights, dims[axis_at] // shards_of).reshape([-1 if axis == axis_at else 1 for axis in range(len(dims))])
    return loudness


def noise(rng, shape, spread, bound, split=(), dtype=jnp.bfloat16):
    loudness = level_of(rng, shape, split, -0.22, 0.18) if split else 1.0
    values = jax.random.normal(rng, shape, jnp.float32) * spread * loudness
    return jnp.minimum(jnp.maximum(values, -bound), bound).astype(dtype)


def setup_inputs(seed: int = 0) -> dict:
    arg_keys = jax.random.split(jax.random.key(seed), 3)
    return {
        "densities": noise(arg_keys[0], (N_IRREP, SOURCES, EXCITE), 1.0, 6.0, ((0, 4), (1, 8)), jnp.float32),
        "reduced_kernel": noise(arg_keys[1], (N_IRREP, TARGETS, SOURCES), SOURCES ** -0.5, 0.125, ((0, 4), (1, 8)), jnp.float32),
    }


def sign_table(count):
    rows_iota = lax.broadcasted_iota(jnp.int32, (count, count), 0)
    cols_iota = lax.broadcasted_iota(jnp.int32, (count, count), 1)
    parity = jnp.zeros((count, count), jnp.int32)
    for level in range(count.bit_length() - 1):
        parity = parity + (rows_iota >> level & 1) * (cols_iota >> level & 1)
    return (1 - 2 * (parity % 2)).astype(jnp.float32)

def apply_tile(operands):
    return jnp.dot(operands[0], operands[1], precision=lax.Precision.HIGHEST, preferred_element_type=jnp.float32)

def reference(densities, reduced_kernel):
    norm_scale = 1.0 / math.sqrt(N_IRREP)
    folded = jnp.einsum('cg,gse->cse', sign_table(N_IRREP), densities, precision=lax.Precision.HIGHEST) * norm_scale
    return lax.map(apply_tile, (reduced_kernel, folded))
```

```python
import functools
import math

import jax
import jax.numpy as jnp
from jax import lax
from jax.experimental import pallas as pl
from jax.experimental.pallas import tpu as pltpu
from jax.sharding import PartitionSpec as P

HIGH = jnp.bfloat16


def exchange(value, axis, bit):
    mask = 1 << bit
    pairs = [(source, source ^ mask) for source in range(lax.axis_size(axis))]
    return lax.ppermute(value, axis, pairs)


def in_two(value):
    high = value.astype(HIGH)
    return high, (value - high.astype(jnp.float32)).astype(HIGH)


def split_kernel(halves, owners, k_ref, high_ref, low_ref):
    width = k_ref.shape[1] // owners // halves
    for owner in range(owners):
        for half in range(halves):
            start = (owner * halves + half) * width
            high, low = in_two(k_ref[:, start : start + width])
            at = (owner // 2) * width
            high_ref[half, owner % 2, :, at : at + width] = high
            low_ref[half, owner % 2, :, at : at + width] = low


def split(k, halves, owners):
    rows, sources = k.shape
    tile = 128
    shape = (halves, 2, rows, sources // halves // 2)
    block = pl.BlockSpec((halves, 2, tile, shape[3]), lambda m: (0, 0, m, 0))
    return pl.pallas_call(
        functools.partial(split_kernel, halves, owners),
        grid=(rows // tile,),
        in_specs=[pl.BlockSpec((tile, sources), lambda m: (m, 0))],
        out_specs=[block, block],
        out_shape=[jax.ShapeDtypeStruct(shape, HIGH)] * 2,
        cost_estimate=pl.CostEstimate(
            flops=4 * rows * sources, bytes_accessed=8 * rows * sources, transcendentals=0
        ),
        compiler_params=pltpu.CompilerParams(vmem_limit_bytes=48 * 2**20),
        name="split_reduced_kernel",
    )(k)


def multiply_kernel(units, depth, pieces, accumulate, me_ref, *refs):
    refs = list(refs)
    highs, lows = refs[:units], refs[units : 2 * units]
    del refs[: 2 * units]
    flat = [[refs.pop(0) for _ in of] for of in pieces]
    before = refs.pop(0) if accumulate else None
    out_ref, f_high, f_low = refs
    me = me_ref[0]

    @pl.when(pl.program_id(0) == 0)
    def _():
        for unit, of in enumerate(pieces):
            for ref, (rels, offset) in zip(flat[unit], of):
                for at, rel in enumerate(rels):
                    high, low = in_two(ref[at])
                    start = ((me ^ rel) >> 1) * depth + offset
                    rows = pl.ds(pl.multiple_of(start, 16), ref.shape[1])
                    f_high[unit, rows, :] = high
                    f_low[unit, rows, :] = low

    total = before[0] if accumulate else None
    for unit in range(units):
        high, low = highs[unit][0, 0], lows[unit][0, 0]
        dot = functools.partial(jnp.dot, preferred_element_type=jnp.float32)
        part = dot(high, f_low[unit]) + dot(low, f_high[unit]) + dot(high, f_high[unit])
        total = part if total is None else total + part
    out_ref[0] = total


def multiply(me, k_high, k_low, units, column, columns, before, accumulate):
    rows, deep = k_high.shape[2:]
    width = units[0][2][0][0].shape[2]
    tile = 256
    depth = 2 * deep // lax.axis_size("row")

    def block(half, core):
        return pl.BlockSpec(
            (1, 1, tile, deep), lambda m, me: (half, (me[0] & 1) ^ core, m, 0)
        )

    blocks = [block(half, core) for half, core, _ in units]
    arrays = [array for _, _, of in units for array, _, _ in of]
    pieces = [[(tuple(rels), offset) for _, rels, offset in of] for _, _, of in units]
    whole = [pl.BlockSpec(a.shape, lambda m, me, n=a.ndim: (0,) * n) for a in arrays]
    place = pl.BlockSpec((1, tile, width), lambda m, me: (0, m, column))
    extra, extra_specs, alias = [], [], {}
    if before is not None:
        extra = [before]
        extra_specs = [place if accumulate else pl.BlockSpec(memory_space=pl.ANY)]
        alias = {1 + 2 * len(units) + len(arrays): 0}

    def kernel(me_ref, *refs):
        refs = list(refs)
        if before is not None and not accumulate:
            del refs[2 * len(units) + len(arrays)]
        multiply_kernel(len(units), depth, pieces, accumulate, me_ref, *refs)

    return pl.pallas_call(
        kernel,
        grid_spec=pltpu.PrefetchScalarGridSpec(
            num_scalar_prefetch=1,
            grid=(rows // tile,),
            in_specs=blocks + blocks + whole + extra_specs,
            out_specs=place,
            scratch_shapes=[pltpu.VMEM((len(units), deep, width), HIGH)] * 2,
        ),
        out_shape=jax.ShapeDtypeStruct((1, rows, columns), jnp.float32),
        input_output_aliases=alias,
        cost_estimate=pl.CostEstimate(
            flops=6 * rows * deep * width * len(units),
            bytes_accessed=4 * rows * deep * len(units) + 4 * rows * width,
            transcendentals=0,
        ),
        compiler_params=pltpu.CompilerParams(vmem_limit_bytes=48 * 2**20),
        name="multiply_sources",
    )(me, *[k_high] * len(units), *[k_low] * len(units), *arrays, *extra)


def fold(holding, levels, order):
    octants = lax.axis_size("irrep")
    octant = lax.axis_index("irrep")
    for step in range(levels):
        bit = (step + order) % levels
        partner = exchange(holding, "irrep", bit)
        upper = octant >> bit & 1
        holding = jnp.where(upper == 1, partner - holding, holding + partner)
    return holding * (1.0 / math.sqrt(octants))


def gather_chips(piece, bits, order):
    rels, held = [0], piece[None]
    for step in range(bits):
        bit = 1 + (step + order) % bits
        held = jnp.concatenate([held, exchange(held, "row", bit)])
        rels = rels + [rel ^ (1 << bit) for rel in rels]
    return held, rels


def body(densities, reduced_kernel):
    owners = lax.axis_size("row")
    levels = lax.axis_size("irrep").bit_length() - 1
    bits = owners.bit_length() - 2
    mine = densities[0]
    deep, columns = mine.shape
    halves, parts = 2, 2
    rows, width = deep // halves, columns // parts
    me = lax.axis_index("row").astype(jnp.int32).reshape(1)

    k_high, k_low = split(reduced_kernel[0], halves, owners)
    out = None
    for part in range(parts):
        units = []
        for half in range(halves):
            chunk = mine[half * rows : (half + 1) * rows, part * width : (part + 1) * width]
            number = part * halves + half
            folded = fold(chunk, levels, 1 if number == 1 else 0)
            if number == parts * halves - 1:
                pieces = [
                    (*gather_chips(folded[: rows // 2], bits, 0), 0),
                    (*gather_chips(folded[rows // 2 :], bits, 1), rows // 2),
                ]
            else:
                pieces = [(*gather_chips(folded, bits, number % 2), 0)]
            other = [
                (exchange(array, "row", 0), [rel ^ 1 for rel in rels], offset)
                for array, rels, offset in pieces
            ]
            units.append((half, 0, pieces))
            units.append((half, 1, other))
        if part < parts - 1:
            out = multiply(me, k_high, k_low, units, part, columns, out, False)
        else:
            out = multiply(me, k_high, k_low, units[:2], part, columns, out, False)
            out = multiply(me, k_high, k_low, units[2:3], part, columns, out, True)
            out = multiply(me, k_high, k_low, units[3:], part, columns, out, True)
    return out


def solution(mesh):
    placed = (P("irrep", "row", None), P("irrep", "row", None))
    return jax.shard_map(
        body, mesh=mesh, in_specs=placed, out_specs=P("irrep", "row", None), check_vma=False
    )
```

```python
import functools
import math

import jax
import jax.numpy as jnp
from jax import lax
from jax.experimental import pallas as pl
from jax.experimental.pallas import tpu as pltpu
from jax.sharding import PartitionSpec as P

HALF = jnp.bfloat16
AXES = ("irrep", "row")


def exchange(value, masks):
    devices = lax.axis_size("irrep") * lax.axis_size("row")
    pairs = [(at, at ^ masks[at & 1]) for at in range(devices)]
    return lax.ppermute(value, AXES, pairs)


def turns(step, count):
    return [(step + core) % count for core in range(2)]


def fold(holding, levels):
    owners, octant = lax.axis_size("row"), lax.axis_index("irrep")
    core = lax.axis_index("row") & 1
    for step in range(levels):
        bits = turns(step, levels)
        partner = exchange(holding, [owners << bit for bit in bits])
        upper = octant >> jnp.where(core == 1, bits[1], bits[0]) & 1
        holding = jnp.where(upper == 1, partner - holding, holding + partner)
    return holding * (1.0 / math.sqrt(lax.axis_size("irrep")))


def gather_chips(piece, bits):
    held = piece[None]
    for step in range(bits):
        masks = [2 << bit for bit in turns(step, bits)]
        held = jnp.concatenate([held, exchange(held, masks)])
    return held


def owner_table(bits):
    me = lax.axis_index("row").astype(jnp.int32)
    core = me & 1
    table = []
    for other in range(2):
        for at in range(1 << bits):
            rel = [other, other]
            for step in range(bits):
                if at >> step & 1:
                    for side, bit in enumerate(turns(step, bits)):
                        rel[side] ^= 2 << bit
            table.append(me ^ jnp.where(core ^ other == 1, rel[1], rel[0]))
    return jnp.stack(table).astype(jnp.int32)


def in_two(value):
    high = value.astype(HALF)
    return high, (value - high.astype(jnp.float32)).astype(HALF)


def multiply_kernel(owners, arrays, accumulate, table_ref, *refs):
    refs = list(refs)
    k_refs = [refs.pop(0) for _ in range(owners)]
    f_refs = [refs.pop(0) for _ in range(arrays)]
    before = refs.pop(0) if accumulate else None
    out_ref, f_high, f_low = refs
    depth = k_refs[0].shape[1]

    @pl.when(pl.program_id(0) == 0)
    def _():
        at = 0
        for ref in f_refs:
            for piece in range(ref.shape[0]):
                high, low = in_two(ref[piece])
                f_high[at : at + depth, :] = high
                f_low[at : at + depth, :] = low
                at += depth

    both = [in_two(ref[...]) for ref in k_refs]
    high = jnp.concatenate([pair[0] for pair in both], axis=1)
    low = jnp.concatenate([pair[1] for pair in both], axis=1)
    dot = functools.partial(jnp.dot, preferred_element_type=jnp.float32)
    total = dot(low, f_high[...]) + dot(high, f_low[...])
    total = total + dot(high, f_high[...])
    if accumulate:
        total = total + before[0]
    out_ref[0] = total


def multiply(table, k, pieces, chunk, chunks, before):
    rows, owners = k.shape[0], sum(array.shape[0] for array in pieces)
    depth, width = pieces[0].shape[1:]
    tile = rows // 3

    def block(piece):
        return pl.BlockSpec(
            (tile, depth), lambda m, table: (m, table[piece] * chunks + chunk)
        )

    whole = [pl.BlockSpec(a.shape, lambda m, table: (0, 0, 0)) for a in pieces]
    place = pl.BlockSpec((1, tile, width), lambda m, table: (0, m, 0))
    accumulate = before is not None
    extra = [before] if accumulate else []
    return pl.pallas_call(
        functools.partial(multiply_kernel, owners, len(pieces), accumulate),
        grid_spec=pltpu.PrefetchScalarGridSpec(
            num_scalar_prefetch=1,
            grid=(rows // tile,),
            in_specs=[block(piece) for piece in range(owners)] + whole + [place] * len(extra),
            out_specs=place,
            scratch_shapes=[pltpu.VMEM((owners * depth, width), HALF)] * 2,
        ),
        out_shape=jax.ShapeDtypeStruct((1, rows, width), jnp.float32),
        input_output_aliases={1 + owners + len(pieces): 0} if accumulate else {},
        cost_estimate=pl.CostEstimate(
            flops=6 * rows * owners * depth * width,
            bytes_accessed=4 * rows * (owners * depth + width),
            transcendentals=0,
        ),
        compiler_params=pltpu.CompilerParams(vmem_limit_bytes=40 * 2**20),
        name="multiply_sources",
    )(table, *[k] * owners, *pieces, *extra)


def body(densities, reduced_kernel):
    levels = lax.axis_size("irrep").bit_length() - 1
    bits = lax.axis_size("row").bit_length() - 2
    mine, k = densities[0], reduced_kernel[0]
    chunks = 2
    depth = mine.shape[0] // chunks
    table = owner_table(bits)
    out = None
    for chunk in range(chunks):
        folded = fold(mine[chunk * depth : (chunk + 1) * depth], levels)
        own = gather_chips(folded, bits)
        other = exchange(own, [1, 1])
        out = multiply(table, k, [own, other], chunk, chunks, out)
    return out


def solution(mesh):
    placed = (P("irrep", "row", None), P("irrep", "row", None))
    return jax.shard_map(
        body, mesh=mesh, in_specs=placed, out_specs=P("irrep", "row", None), check_vma=False
    )
```

```python
import functools
import math

import jax
import jax.numpy as jnp
from jax import lax
from jax.experimental import pallas as pl
from jax.experimental.pallas import tpu as pltpu
from jax.sharding import PartitionSpec as P

HALF = jnp.bfloat16
AXES = ("irrep", "row")


def exchange(value, masks):
    devices = lax.axis_size("irrep") * lax.axis_size("row")
    pairs = [(at, at ^ masks[at & 1]) for at in range(devices)]
    return lax.ppermute(value, AXES, pairs)


def turns(step, count):
    return [(step + core) % count for core in range(2)]


def fold(holding, step, levels, beside=None):
    owners, octant = lax.axis_size("row"), lax.axis_index("irrep")
    core = lax.axis_index("row") & 1
    bits = turns(step, levels)
    partner = exchange(holding, [owners << bit for bit in bits])
    if beside is not None:
        partner, beside = lax.optimization_barrier((partner, beside))
    upper = octant >> jnp.where(core == 1, bits[1], bits[0]) & 1
    holding = jnp.where(upper == 1, partner - holding, holding + partner)
    if step == levels - 1:
        holding = holding * (1.0 / math.sqrt(lax.axis_size("irrep")))
    return holding if beside is None else (holding, beside)


def gather_chips(piece, bits):
    held = piece[None]
    for step in range(bits):
        masks = [2 << bit for bit in turns(step, bits)]
        held = jnp.concatenate([held, exchange(held, masks)])
    return held


def owner_table(bits):
    me = lax.axis_index("row").astype(jnp.int32)
    core = me & 1
    table = []
    for other in range(2):
        for at in range(1 << bits):
            rel = [other, other]
            for step in range(bits):
                if at >> step & 1:
                    for side, bit in enumerate(turns(step, bits)):
                        rel[side] ^= 2 << bit
            table.append(me ^ jnp.where(core ^ other == 1, rel[1], rel[0]))
    return jnp.stack(table).astype(jnp.int32)


def in_two(value):
    high = value.astype(HALF)
    return high, (value - high.astype(jnp.float32)).astype(HALF)


def split_kernel(owners, chunks, table_ref, k_ref, high_ref, low_ref):
    depth = k_ref.shape[1] // owners // chunks
    for chunk in range(chunks):
        for piece in range(owners):
            start = (table_ref[piece] * chunks + chunk) * depth
            high, low = in_two(k_ref[:, pl.ds(pl.multiple_of(start, depth), depth)])
            at = (chunk * owners + piece) * depth
            high_ref[:, at : at + depth] = high
            low_ref[:, at : at + depth] = low


def split(table, k, chunks):
    rows, sources = k.shape
    tile = rows // 6
    block = pl.BlockSpec((tile, sources), lambda m, table: (m, 0))
    return pl.pallas_call(
        functools.partial(split_kernel, lax.axis_size("row"), chunks),
        grid_spec=pltpu.PrefetchScalarGridSpec(
            num_scalar_prefetch=1,
            grid=(rows // tile,),
            in_specs=[block],
            out_specs=[block, block],
        ),
        out_shape=[pltpu.VMEM((rows, sources), HALF)] * 2,
        cost_estimate=pl.CostEstimate(
            flops=4 * rows * sources, bytes_accessed=4 * rows * sources, transcendentals=0
        ),
        compiler_params=pltpu.CompilerParams(vmem_limit_bytes=12 * 2**20),
        name="split_reduced_kernel",
    )(table, k)


def multiply_kernel(chunk, arrays, last, high_ref, low_ref, *refs):
    refs = list(refs)
    f_refs = [refs.pop(0) for _ in range(arrays)]
    before = refs.pop(0) if last else None
    out_ref, f_high, f_low = refs[:3]
    depth = f_refs[0].shape[1]
    at = 0
    for ref in f_refs:
        for piece in range(ref.shape[0]):
            high, low = in_two(ref[piece])
            f_high[at : at + depth, :] = high
            f_low[at : at + depth, :] = low
            at += depth
    columns = slice(chunk * at, (chunk + 1) * at)
    rows = high_ref.shape[0]
    tile = rows // 3

    def product(step):
        here = pl.ds(pl.multiple_of(step * tile, tile), tile)
        high, low = high_ref[here, columns], low_ref[here, columns]
        left = jnp.concatenate([low, high, high], axis=1)
        right = jnp.concatenate([f_high[...], f_low[...], f_high[...]], axis=0)
        return here, jnp.dot(left, right, preferred_element_type=jnp.float32)

    if not last:

        @pl.loop(0, rows // tile)
        def _(step):
            here, total = product(step)
            out_ref[here, :] = total

    else:
        result, sems = refs[3:]

        @pl.loop(0, rows // tile)
        def _(step):
            here, total = product(step)
            result[here, :] = total + before[here, :]
            pltpu.make_async_copy(
                result.at[here, :], out_ref.at[0, here, :], sems.at[step]
            ).start()

        for step in range(rows // tile):
            here = slice(step * tile, (step + 1) * tile)
            pltpu.make_async_copy(
                result.at[here, :], out_ref.at[0, here, :], sems.at[step]
            ).wait()


def multiply(k_high, k_low, pieces, chunk, before, last):
    rows = k_high.shape[0]
    count, (depth, width) = sum(a.shape[0] for a in pieces), pieces[0].shape[1:]
    vmem = pl.BlockSpec(memory_space=pltpu.VMEM)
    operands = [k_high, k_low, *pieces] + ([before] if last else [])
    scratch = [pltpu.VMEM((count * depth, width), HALF)] * 2
    if last:
        scratch += [pltpu.VMEM((rows, width), jnp.float32), pltpu.SemaphoreType.DMA((3,))]
        out_shape = jax.ShapeDtypeStruct((1, rows, width), jnp.float32)
    else:
        out_shape = pltpu.VMEM((rows, width), jnp.float32)
    held = [pltpu.with_memory_space_constraint(a, pltpu.VMEM) for a in operands]
    return pl.pallas_call(
        functools.partial(multiply_kernel, chunk, len(pieces), last),
        in_specs=[vmem] * len(operands),
        out_specs=pl.BlockSpec(memory_space=pl.ANY) if last else vmem,
        out_shape=out_shape,
        scratch_shapes=scratch,
        cost_estimate=pl.CostEstimate(
            flops=6 * rows * count * depth * width,
            bytes_accessed=4 * rows * (count * depth + width),
            transcendentals=0,
        ),
        compiler_params=pltpu.CompilerParams(vmem_limit_bytes=24 * 2**20),
        name="multiply_sources",
    )(*held)


def body(densities, reduced_kernel):
    levels = lax.axis_size("irrep").bit_length() - 1
    bits = lax.axis_size("row").bit_length() - 2
    chunks = 2
    parts = split(owner_table(bits), reduced_kernel[0], chunks)
    mine, (k_high, k_low) = fold(densities[0], 0, levels, tuple(parts))
    depth = mine.shape[0] // chunks
    out = None
    for chunk in range(chunks):
        folded = lax.optimization_barrier(mine[chunk * depth : (chunk + 1) * depth])
        for step in range(1, levels):
            folded = fold(folded, step, levels)
        own = gather_chips(folded, bits)
        if out is not None:
            own, out = lax.optimization_barrier((own, out))
        other = exchange(own, [1, 1])
        out = multiply(k_high, k_low, [own, other], chunk, out, chunk == chunks - 1)
    return out


def solution(mesh):
    placed = (P("irrep", "row", None), P("irrep", "row", None))
    return jax.shard_map(
        body, mesh=mesh, in_specs=placed, out_specs=P("irrep", "row", None), check_vma=False
    )
```

```python
import functools
import math

import jax
import jax.numpy as jnp
from jax import lax
from jax.experimental import pallas as pl
from jax.experimental.pallas import tpu as pltpu
from jax.sharding import PartitionSpec as P

HALF = jnp.bfloat16
AXES = ("irrep", "row")
TILES = 3
WEIGHTS = ((0.1, 0.1), (0.1, 0.1))


def exchange(value, masks):
    devices = lax.axis_size("irrep") * lax.axis_size("row")
    pairs = [(at, at ^ masks[at & 1]) for at in range(devices)]
    return lax.ppermute(value, AXES, pairs)


def turns(step, count):
    return [(step + core) % count for core in range(2)]


def across(held, step, bits):
    return exchange(held, [2 << bit for bit in turns(step, bits)])


def gather_chips(held, steps, bits):
    for step in steps:
        held = jnp.concatenate([held, across(held, step, bits)])
    return held


def numbers(levels, bits):
    me = lax.axis_index("row").astype(jnp.int32)
    octant = lax.axis_index("irrep").astype(jnp.int32)
    core = me & 1
    half = 1 << (bits - 1)
    table = []
    for group in range(2):
        for other in range(2):
            for at in range(group * half, (group + 1) * half):
                rel = [other, other]
                for step in range(bits):
                    if at >> step & 1:
                        for side, bit in enumerate(turns(step, bits)):
                            rel[side] ^= 2 << bit
                table.append(me ^ jnp.where(core ^ other == 1, rel[1], rel[0]))
    for step in range(levels):
        bit = turns(step, levels)
        table.append(octant >> jnp.where(core == 1, bit[1], bit[0]) & 1)
    return jnp.stack(table).astype(jnp.int32)


def cost(microseconds):
    return pl.CostEstimate(
        flops=int(microseconds * 1.15e9), bytes_accessed=0, transcendentals=0
    )


VMEM = pl.BlockSpec(memory_space=pltpu.VMEM)
SMEM = pl.BlockSpec(memory_space=pltpu.SMEM)


def fold_kernel(at, scale, table_ref, holding_ref, partner_ref, out_ref):
    sign = jnp.where(table_ref[at] == 1, -1.0, 1.0)
    total = partner_ref[...] + sign * holding_ref[...]
    out_ref[...] = total if scale is None else total * scale


def fold(table, holding, partner, step, levels, weight):
    last = step == levels - 1
    scale = 1.0 / math.sqrt(lax.axis_size("irrep")) if last else None
    at = lax.axis_size("row") + step
    return pl.pallas_call(
        functools.partial(fold_kernel, at, scale),
        in_specs=[SMEM, VMEM, VMEM],
        out_specs=VMEM,
        out_shape=pltpu.VMEM(holding.shape, jnp.float32),
        cost_estimate=cost(weight),
        compiler_params=pltpu.CompilerParams(vmem_limit_bytes=2 * 2**20),
        name="fold_step",
    )(table, holding, partner)


def partner_of(holding, step, levels):
    owners = lax.axis_size("row")
    return exchange(holding, [owners << bit for bit in turns(step, levels)])


def in_two(value):
    high = value.astype(HALF)
    return high, (value - high.astype(jnp.float32)).astype(HALF)


def split_kernel(owners, chunks, table_ref, k_ref, high_ref, low_ref):
    depth = k_ref.shape[1] // owners // chunks
    for chunk in range(chunks):
        for piece in range(owners):
            start = (table_ref[piece] * chunks + chunk) * depth
            high, low = in_two(k_ref[:, pl.ds(pl.multiple_of(start, depth), depth)])
            at = (chunk * owners + piece) * depth
            high_ref[:, at : at + depth] = high
            low_ref[:, at : at + depth] = low


def split(table, k, chunks):
    rows, sources = k.shape
    tile = rows // 6
    block = pl.BlockSpec((tile, sources), lambda m, table: (m, 0))
    return pl.pallas_call(
        functools.partial(split_kernel, lax.axis_size("row"), chunks),
        grid_spec=pltpu.PrefetchScalarGridSpec(
            num_scalar_prefetch=1,
            grid=(rows // tile,),
            in_specs=[block],
            out_specs=[block, block],
        ),
        out_shape=[pltpu.VMEM((rows, sources), HALF)] * 2,
        cost_estimate=pl.CostEstimate(
            flops=4 * rows * sources, bytes_accessed=4 * rows * sources, transcendentals=0
        ),
        compiler_params=pltpu.CompilerParams(vmem_limit_bytes=18 * 2**20),
        name="split_reduced_kernel",
    )(table, pltpu.with_memory_space_constraint(k, pltpu.HBM))


def multiply_kernel(block, arrays, accumulate, last, high_ref, low_ref, *refs):
    refs = list(refs)
    f_refs = [refs.pop(0) for _ in range(arrays)]
    before = refs.pop(0) if accumulate else None
    out_ref, f_high, f_low = refs[:3]
    depth = f_refs[0].shape[1]
    at = 0
    for ref in f_refs:
        for piece in range(ref.shape[0]):
            high, low = in_two(ref[piece])
            f_high[at : at + depth, :] = high
            f_low[at : at + depth, :] = low
            at += depth
    sources = slice(block * at, (block + 1) * at)
    tile = high_ref.shape[0] // TILES

    def product(step):
        here = pl.ds(pl.multiple_of(step * tile, tile), tile)
        high, low = high_ref[here, sources], low_ref[here, sources]
        left = jnp.concatenate([low, high, high], axis=1)
        right = jnp.concatenate([f_high[...], f_low[...], f_high[...]], axis=0)
        total = jnp.dot(left, right, preferred_element_type=jnp.float32)
        return here, total + before[here, :] if accumulate else total

    if not last:

        @pl.loop(0, TILES)
        def _(step):
            here, total = product(step)
            out_ref[here, :] = total

    else:
        result, sems = refs[3:]

        def copy(here, step):
            return pltpu.make_async_copy(
                result.at[here, :], out_ref.at[0, here, :], sems.at[step]
            )

        @pl.loop(0, TILES)
        def _(step):
            here, total = product(step)
            result[here, :] = total
            copy(here, step).start()

        for step in range(TILES):
            copy(slice(step * tile, (step + 1) * tile), step).wait()


def multiply(k_high, k_low, pieces, block, before, last):
    rows = k_high.shape[0]
    count, (depth, width) = sum(a.shape[0] for a in pieces), pieces[0].shape[1:]
    accumulate = before is not None
    operands = [k_high, k_low, *pieces] + ([before] if accumulate else [])
    operands = [pltpu.with_memory_space_constraint(a, pltpu.VMEM) for a in operands]
    scratch = [pltpu.VMEM((count * depth, width), HALF)] * 2
    alias = {}
    if last:
        scratch += [pltpu.VMEM((rows, width), jnp.float32), pltpu.SemaphoreType.DMA((TILES,))]
        shape = jax.ShapeDtypeStruct((1, rows, width), jnp.float32)
    else:
        shape = pltpu.VMEM((rows, width), jnp.float32)
        alias = {len(operands) - 1: 0} if accumulate else {}
    return pl.pallas_call(
        functools.partial(multiply_kernel, block, len(pieces), accumulate, last),
        in_specs=[VMEM] * len(operands),
        out_specs=pl.BlockSpec(memory_space=pl.ANY) if last else VMEM,
        out_shape=shape,
        input_output_aliases=alias,
        scratch_shapes=scratch,
        cost_estimate=pl.CostEstimate(
            flops=6 * rows * count * depth * width, bytes_accessed=0, transcendentals=0
        ),
        compiler_params=pltpu.CompilerParams(vmem_limit_bytes=14 * 2**20),
        name="multiply_sources",
    )(*operands)


def after(value, others):
    return lax.optimization_barrier((value, others))[0]


def body(densities, reduced_kernel):
    levels = lax.axis_size("irrep").bit_length() - 1
    bits = lax.axis_size("row").bit_length() - 2
    mine = densities[0]
    half, width = mine.shape[0] // 2, mine.shape[1]
    table = numbers(levels, bits)
    ks = split(table, reduced_kernel[0], 2)
    parts = [mine[at * half : (at + 1) * half] for at in range(2)]
    for step in range(levels):
        partners = [partner_of(part, step, levels) for part in parts]
        if step == 0:
            partners[0] = after(partners[0], tuple(ks))
        else:
            partners[0] = after(partners[0], parts[1])
        parts = [
            fold(table, *pair, step, levels, WEIGHTS[step > 0][at])
            for at, pair in enumerate(zip(parts, partners))
        ]
    early = gather_chips(parts[0][None], range(bits - 1), bits)
    early = after(early, parts[1])
    late = gather_chips(parts[1][None], range(bits - 1), bits)
    arrived = across(early, bits - 1, bits)
    arrived = after(arrived, late)
    out = multiply(*ks, [early, exchange(early, [1, 1])], 0, None, False)
    out = multiply(*ks, [late, exchange(late, [1, 1])], 2, out, False)
    out = multiply(*ks, [arrived, exchange(arrived, [1, 1])], 1, out, False)
    arrived = across(late, bits - 1, bits)
    arrived = after(arrived, out)
    return multiply(*ks, [arrived, exchange(arrived, [1, 1])], 3, out, True)


def solution(mesh):
    placed = (P("irrep", "row", None), P("irrep", "row", None))
    return jax.shard_map(
        body, mesh=mesh, in_specs=placed, out_specs=P("irrep", "row", None), check_vma=False
    )
```

```python
import functools
import math

import jax
import jax.numpy as jnp
from jax import lax
from jax.experimental import pallas as pl
from jax.experimental.pallas import tpu as pltpu
from jax.sharding import PartitionSpec as P

HALF = jnp.bfloat16
AXES = ("irrep", "row")
TILES = 3


def exchange(value, masks):
    devices = lax.axis_size("irrep") * lax.axis_size("row")
    pairs = [(at, at ^ masks[at & 1]) for at in range(devices)]
    return lax.ppermute(value, AXES, pairs)


def turns(step, count):
    return [(step + core) % count for core in range(2)]


def across(held, step, bits):
    return exchange(held, [2 << bit for bit in turns(step, bits)])


def gather_chips(held, steps, bits, others=None):
    for step in steps:
        held = jnp.concatenate([held, after(across(held, step, bits), others)])
    return held


def numbers(levels, bits):
    me = lax.axis_index("row").astype(jnp.int32)
    octant = lax.axis_index("irrep").astype(jnp.int32)
    core = me & 1
    half = 1 << (bits - 1)
    table = []
    for group in range(2):
        for other in range(2):
            for at in range(group * half, (group + 1) * half):
                rel = [other, other]
                for step in range(bits):
                    if at >> step & 1:
                        for side, bit in enumerate(turns(step, bits)):
                            rel[side] ^= 2 << bit
                table.append(me ^ jnp.where(core ^ other == 1, rel[1], rel[0]))
    signs = []
    for step in range(levels):
        bit = turns(step, levels)
        upper = octant >> jnp.where(core == 1, bit[1], bit[0]) & 1
        signs.append((1 - 2 * upper).astype(jnp.float32))
    return lax.optimization_barrier((jnp.stack(table).astype(jnp.int32), signs))


VMEM = pl.BlockSpec(memory_space=pltpu.VMEM)
SMEM = pl.BlockSpec(memory_space=pltpu.SMEM)
ANY = pl.BlockSpec(memory_space=pl.ANY)


def fold(holding, partner, sign, step, levels):
    total = partner + sign * holding
    if step == levels - 1:
        total = total * (1.0 / math.sqrt(lax.axis_size("irrep")))
    return lax.optimization_barrier(total)


def partner_of(holding, step, levels):
    owners = lax.axis_size("row")
    return exchange(holding, [owners << bit for bit in turns(step, levels)])


def in_two(value):
    high = value.astype(HALF)
    return high, (value - high.astype(jnp.float32)).astype(HALF)


def split_kernel(owners, chunks, table_ref, k_ref, high_ref, low_ref, buffers, sems):
    count, tile, sources = buffers.shape
    depth = sources // owners // chunks
    steps = k_ref.shape[0] // tile

    def fetch(step):
        here = pl.ds(pl.multiple_of(step * tile, tile), tile)
        slot = lax.rem(step, count)
        return pltpu.make_async_copy(k_ref.at[here, :], buffers.at[slot], sems.at[slot])

    for step in range(count - 1):
        fetch(step).start()

    @pl.loop(0, steps)
    def _(step):
        fetch(step).wait()

        @pl.when(step + count - 1 < steps)
        def _():
            fetch(step + count - 1).start()

        slot = lax.rem(step, count)
        here = pl.ds(pl.multiple_of(step * tile, tile), tile)
        for chunk in range(chunks):
            for piece in range(owners):
                start = (table_ref[piece] * chunks + chunk) * depth
                columns = pl.ds(pl.multiple_of(start, depth), depth)
                high, low = in_two(buffers[slot, :, columns])
                at = (chunk * owners + piece) * depth
                high_ref[here, at : at + depth] = high
                low_ref[here, at : at + depth] = low


def split(table, k, chunks):
    rows, sources = k.shape
    count, tile = 3, rows // 6
    return pl.pallas_call(
        functools.partial(split_kernel, lax.axis_size("row"), chunks),
        in_specs=[SMEM, ANY],
        out_specs=[VMEM, VMEM],
        out_shape=[pltpu.VMEM((rows, sources), HALF)] * 2,
        scratch_shapes=[
            pltpu.VMEM((count, tile, sources), jnp.float32),
            pltpu.SemaphoreType.DMA((count,)),
        ],
        cost_estimate=pl.CostEstimate(
            flops=4 * rows * sources, bytes_accessed=4 * rows * sources, transcendentals=0
        ),
        compiler_params=pltpu.CompilerParams(vmem_limit_bytes=18 * 2**20),
        name="split_reduced_kernel",
    )(table, pltpu.with_memory_space_constraint(k, pltpu.HBM))


def multiply_kernel(block, arrays, accumulate, last, high_ref, low_ref, *refs):
    refs = list(refs)
    f_refs = [refs.pop(0) for _ in range(arrays)]
    before = refs.pop(0) if accumulate else None
    out_ref, f_high, f_low = refs[:3]
    depth = f_refs[0].shape[1]
    at = 0
    for ref in f_refs:
        for piece in range(ref.shape[0]):
            high, low = in_two(ref[piece])
            f_high[at : at + depth, :] = high
            f_low[at : at + depth, :] = low
            at += depth
    sources = slice(block * at, (block + 1) * at)
    tile = high_ref.shape[0] // TILES

    def product(step):
        here = pl.ds(pl.multiple_of(step * tile, tile), tile)
        high, low = high_ref[here, sources], low_ref[here, sources]
        left = jnp.concatenate([low, high, high], axis=1)
        right = jnp.concatenate([f_high[...], f_low[...], f_high[...]], axis=0)
        total = jnp.dot(left, right, preferred_element_type=jnp.float32)
        return here, total + before[here, :] if accumulate else total

    if not last:

        @pl.loop(0, TILES)
        def _(step):
            here, total = product(step)
            out_ref[here, :] = total

    else:
        result, sems = refs[3:]

        def copy(here, step):
            return pltpu.make_async_copy(
                result.at[here, :], out_ref.at[0, here, :], sems.at[step]
            )

        @pl.loop(0, TILES)
        def _(step):
            here, total = product(step)
            result[here, :] = total
            copy(here, step).start()

        for step in range(TILES):
            copy(slice(step * tile, (step + 1) * tile), step).wait()


def multiply(k_high, k_low, pieces, block, before, last):
    rows = k_high.shape[0]
    count, (depth, width) = sum(a.shape[0] for a in pieces), pieces[0].shape[1:]
    accumulate = before is not None
    operands = [k_high, k_low, *pieces] + ([before] if accumulate else [])
    operands = [pltpu.with_memory_space_constraint(a, pltpu.VMEM) for a in operands]
    scratch = [pltpu.VMEM((count * depth, width), HALF)] * 2
    alias = {}
    if last:
        scratch += [pltpu.VMEM((rows, width), jnp.float32), pltpu.SemaphoreType.DMA((TILES,))]
        shape = jax.ShapeDtypeStruct((1, rows, width), jnp.float32)
    else:
        shape = pltpu.VMEM((rows, width), jnp.float32)
        alias = {len(operands) - 1: 0} if accumulate else {}
    return pl.pallas_call(
        functools.partial(multiply_kernel, block, len(pieces), accumulate, last),
        in_specs=[VMEM] * len(operands),
        out_specs=ANY if last else VMEM,
        out_shape=shape,
        input_output_aliases=alias,
        scratch_shapes=scratch,
        cost_estimate=pl.CostEstimate(
            flops=6 * rows * count * depth * width, bytes_accessed=0, transcendentals=0
        ),
        compiler_params=pltpu.CompilerParams(vmem_limit_bytes=14 * 2**20),
        name="multiply_sources",
    )(*operands)


def after(value, others):
    return value if others is None else lax.optimization_barrier((value, others))[0]


def body(densities, reduced_kernel):
    levels = lax.axis_size("irrep").bit_length() - 1
    bits = lax.axis_size("row").bit_length() - 2
    mine = densities[0]
    half = mine.shape[0] // 2
    table, signs = numbers(levels, bits)
    ks = split(table, reduced_kernel[0], 2)
    parts = [lax.optimization_barrier(mine[at * half : (at + 1) * half]) for at in range(2)]
    for step in range(levels):
        partners = [partner_of(part, step, levels) for part in parts]
        partners[0] = after(partners[0], tuple(ks) if step == 0 else parts[1])
        parts = [fold(*pair, signs[step], step, levels) for pair in zip(parts, partners)]
    last = bits - 1
    early = gather_chips(parts[0][None], range(last), bits)
    early = after(early, parts[1])
    arrived = across(early, last, bits)
    out = multiply(*ks, [early, exchange(early, [1, 1])], 0, None, False)
    late = gather_chips(parts[1][None], range(last), bits, out)
    out = multiply(*ks, [after(late, arrived), exchange(late, [1, 1])], 2, out, False)
    out = multiply(*ks, [arrived, exchange(arrived, [1, 1])], 1, out, False)
    arrived = after(across(late, last, bits), out)
    return multiply(*ks, [arrived, exchange(arrived, [1, 1])], 3, out, True)


def solution(mesh):
    placed = (P("irrep", "row", None), P("irrep", "row", None))
    return jax.shard_map(
        body, mesh=mesh, in_specs=placed, out_specs=P("irrep", "row", None), check_vma=False
    )
```

```python
import functools
import math

import jax
import jax.numpy as jnp
from jax import lax
from jax.experimental import pallas as pl
from jax.experimental.pallas import tpu as pltpu
from jax.sharding import PartitionSpec as P

HALF = jnp.bfloat16
AXES = ("irrep", "row")
TILES = 3
WEIGHT = 6


def exchange(value, masks):
    devices = lax.axis_size("irrep") * lax.axis_size("row")
    pairs = [(at, at ^ masks[at & 1]) for at in range(devices)]
    return lax.ppermute(value, AXES, pairs)


def turns(step, count):
    return [(step + core) % count for core in range(2)]


def across(held, step, bits):
    return exchange(held, [2 << bit for bit in turns(step, bits)])


def swapped(held, parts):
    size = held.shape[0] // parts
    return [exchange(held[at : at + size], [1, 1]) for at in range(0, held.shape[0], size)]


def gather_chips(held, steps, bits, others=None):
    for step in steps:
        held = jnp.concatenate([held, after(across(held, step, bits), others)])
    return held


def numbers(levels, bits):
    me = lax.axis_index("row").astype(jnp.int32)
    octant = lax.axis_index("irrep").astype(jnp.int32)
    core = me & 1
    half = 1 << (bits - 1)
    table = []
    for group in range(2):
        for other in range(2):
            for at in range(group * half, (group + 1) * half):
                rel = [other, other]
                for step in range(bits):
                    if at >> step & 1:
                        for side, bit in enumerate(turns(step, bits)):
                            rel[side] ^= 2 << bit
                table.append(me ^ jnp.where(core ^ other == 1, rel[1], rel[0]))
    signs = []
    for step in range(levels):
        bit = turns(step, levels)
        upper = octant >> jnp.where(core == 1, bit[1], bit[0]) & 1
        signs.append((1 - 2 * upper).astype(jnp.float32))
    return lax.optimization_barrier((jnp.stack(table).astype(jnp.int32), signs))


VMEM = pl.BlockSpec(memory_space=pltpu.VMEM)
SMEM = pl.BlockSpec(memory_space=pltpu.SMEM)
ANY = pl.BlockSpec(memory_space=pl.ANY)


def fold(holding, partner, sign, step, levels):
    total = partner + sign * holding
    if step == levels - 1:
        total = total * (1.0 / math.sqrt(lax.axis_size("irrep")))
    return lax.optimization_barrier(total)


def partner_of(holding, step, levels):
    owners = lax.axis_size("row")
    return exchange(holding, [owners << bit for bit in turns(step, levels)])


def in_two(value):
    high = value.astype(HALF)
    return high, (value - high.astype(jnp.float32)).astype(HALF)


def split_kernel(owners, chunks, table_ref, k_ref, high_ref, low_ref, buffers, sems):
    count, tile, sources = buffers.shape
    depth = sources // owners // chunks
    steps = k_ref.shape[0] // tile

    def fetch(step):
        here = pl.ds(pl.multiple_of(step * tile, tile), tile)
        slot = lax.rem(step, count)
        return pltpu.make_async_copy(k_ref.at[here, :], buffers.at[slot], sems.at[slot])

    for step in range(count - 1):
        fetch(step).start()

    @pl.loop(0, steps)
    def _(step):
        fetch(step).wait()

        @pl.when(step + count - 1 < steps)
        def _():
            fetch(step + count - 1).start()

        slot = lax.rem(step, count)
        here = pl.ds(pl.multiple_of(step * tile, tile), tile)
        for chunk in range(chunks):
            for piece in range(owners):
                start = (table_ref[piece] * chunks + chunk) * depth
                columns = pl.ds(pl.multiple_of(start, depth), depth)
                high, low = in_two(buffers[slot, :, columns])
                at = (chunk * owners + piece) * depth
                high_ref[here, at : at + depth] = high
                low_ref[here, at : at + depth] = low


def split(table, k, chunks):
    rows, sources = k.shape
    count, tile = 3, rows // 6
    return pl.pallas_call(
        functools.partial(split_kernel, lax.axis_size("row"), chunks),
        in_specs=[SMEM, ANY],
        out_specs=[VMEM, VMEM],
        out_shape=[pltpu.VMEM((rows, sources), HALF)] * 2,
        scratch_shapes=[
            pltpu.VMEM((count, tile, sources), jnp.float32),
            pltpu.SemaphoreType.DMA((count,)),
        ],
        cost_estimate=pl.CostEstimate(
            flops=4 * rows * sources, bytes_accessed=4 * rows * sources, transcendentals=0
        ),
        compiler_params=pltpu.CompilerParams(vmem_limit_bytes=18 * 2**20),
        name="split_reduced_kernel",
    )(table, pltpu.with_memory_space_constraint(k, pltpu.HBM))


def multiply_kernel(start, arrays, accumulate, last, high_ref, low_ref, *refs):
    refs = list(refs)
    f_refs = [refs.pop(0) for _ in range(arrays)]
    before = refs.pop(0) if accumulate else None
    out_ref, f_high, f_low = refs[:3]
    depth = f_refs[0].shape[1]
    at = 0
    for ref in f_refs:
        for piece in range(ref.shape[0]):
            high, low = in_two(ref[piece])
            f_high[at : at + depth, :] = high
            f_low[at : at + depth, :] = low
            at += depth
    sources = slice(start * depth, start * depth + at)
    tile = high_ref.shape[0] // TILES

    def product(step):
        here = pl.ds(pl.multiple_of(step * tile, tile), tile)
        high, low = high_ref[here, sources], low_ref[here, sources]
        left = jnp.concatenate([low, high, high], axis=1)
        right = jnp.concatenate([f_high[...], f_low[...], f_high[...]], axis=0)
        total = jnp.dot(left, right, preferred_element_type=jnp.float32)
        return here, total + before[here, :] if accumulate else total

    if not last:

        @pl.loop(0, TILES)
        def _(step):
            here, total = product(step)
            out_ref[here, :] = total

    else:
        result, sems = refs[3:]

        def copy(here, step):
            return pltpu.make_async_copy(
                result.at[here, :], out_ref.at[0, here, :], sems.at[step]
            )

        @pl.loop(0, TILES)
        def _(step):
            here, total = product(step)
            result[here, :] = total
            copy(here, step).start()

        for step in range(TILES):
            copy(slice(step * tile, (step + 1) * tile), step).wait()


def multiply(k_high, k_low, pieces, start, before, last=False):
    rows = k_high.shape[0]
    count, (depth, width) = sum(a.shape[0] for a in pieces), pieces[0].shape[1:]
    accumulate = before is not None
    operands = [k_high, k_low, *pieces] + ([before] if accumulate else [])
    operands = [pltpu.with_memory_space_constraint(a, pltpu.VMEM) for a in operands]
    scratch = [pltpu.VMEM((count * depth, width), HALF)] * 2
    alias = {}
    if last:
        scratch += [pltpu.VMEM((rows, width), jnp.float32), pltpu.SemaphoreType.DMA((TILES,))]
        shape = jax.ShapeDtypeStruct((1, rows, width), jnp.float32)
    else:
        shape = pltpu.VMEM((rows, width), jnp.float32)
        alias = {len(operands) - 1: 0} if accumulate else {}
    return pl.pallas_call(
        functools.partial(multiply_kernel, start, len(pieces), accumulate, last),
        in_specs=[VMEM] * len(operands),
        out_specs=ANY if last else VMEM,
        out_shape=shape,
        input_output_aliases=alias,
        scratch_shapes=scratch,
        cost_estimate=pl.CostEstimate(
            flops=int(WEIGHT * rows * count * depth * width), bytes_accessed=0, transcendentals=0
        ),
        compiler_params=pltpu.CompilerParams(vmem_limit_bytes=14 * 2**20),
        name="multiply_sources",
    )(*operands)


def after(value, others):
    return value if others is None else lax.optimization_barrier((value, others))[0]


def body(densities, reduced_kernel):
    levels = lax.axis_size("irrep").bit_length() - 1
    bits = lax.axis_size("row").bit_length() - 2
    mine = densities[0]
    half = mine.shape[0] // 2
    table, signs = numbers(levels, bits)
    ks = split(table, reduced_kernel[0], 2)
    parts = [lax.optimization_barrier(mine[at * half : (at + 1) * half]) for at in range(2)]
    for step in range(levels):
        partners = [partner_of(part, step, levels) for part in parts]
        partners[0] = after(partners[0], tuple(ks) if step == 0 else parts[1])
        parts = [fold(*pair, signs[step], step, levels) for pair in zip(parts, partners)]
    last = bits - 1
    group = lax.axis_size("row") // 2
    early = gather_chips(parts[0][None], range(last), bits)
    early = after(early, parts[1])
    arrived = across(early, last, bits)
    out = multiply(*ks, [early, exchange(early, [1, 1])], 0, None)
    late = gather_chips(parts[1][None], range(last), bits, out)
    out = multiply(*ks, [late, exchange(late, [1, 1])], 2 * group, out)
    out = multiply(*ks, [arrived, *swapped(arrived, 2)], group, out)
    arrived = after(across(late, last, bits), out)
    out = multiply(*ks, [arrived], 3 * group, out)
    return multiply(*ks, [exchange(arrived, [1, 1])], 3 * group + group // 2, out, True)


def solution(mesh):
    placed = (P("irrep", "row", None), P("irrep", "row", None))
    return jax.shard_map(
        body, mesh=mesh, in_specs=placed, out_specs=P("irrep", "row", None), check_vma=False
    )
```

```python
import functools
import math

import jax
import jax.numpy as jnp
from jax import lax
from jax.experimental import pallas as pl
from jax.experimental.pallas import tpu as pltpu
from jax.sharding import PartitionSpec as P

HALF = jnp.bfloat16
AXES = ("irrep", "row")
TILES = 2
WEIGHT = 6


def exchange(value, masks):
    devices = lax.axis_size("irrep") * lax.axis_size("row")
    pairs = [(at, at ^ masks[at & 1]) for at in range(devices)]
    return lax.ppermute(value, AXES, pairs)


def turns(step, count):
    return [(step + core) % count for core in range(2)]


def across(held, step, bits):
    return exchange(held, [2 << bit for bit in turns(step, bits)])


def swapped(held, parts):
    size = held.shape[0] // parts
    return [exchange(held[at : at + size], [1, 1]) for at in range(0, held.shape[0], size)]


def gather_chips(held, steps, bits, others=None):
    for step in steps:
        held = jnp.concatenate([held, after(across(held, step, bits), others)])
    return held


def numbers(levels, bits):
    me = lax.axis_index("row").astype(jnp.int32)
    octant = lax.axis_index("irrep").astype(jnp.int32)
    core = me & 1
    half = 1 << (bits - 1)
    table = []
    for group in range(2):
        for other in range(2):
            for at in range(group * half, (group + 1) * half):
                rel = [other, other]
                for step in range(bits):
                    if at >> step & 1:
                        for side, bit in enumerate(turns(step, bits)):
                            rel[side] ^= 2 << bit
                table.append(me ^ jnp.where(core ^ other == 1, rel[1], rel[0]))
    signs = []
    for step in range(levels):
        bit = turns(step, levels)
        upper = octant >> jnp.where(core == 1, bit[1], bit[0]) & 1
        signs.append((1 - 2 * upper).astype(jnp.float32))
    return lax.optimization_barrier((jnp.stack(table).astype(jnp.int32), signs))


VMEM = pl.BlockSpec(memory_space=pltpu.VMEM)
SMEM = pl.BlockSpec(memory_space=pltpu.SMEM)
ANY = pl.BlockSpec(memory_space=pl.ANY)


def fold(holding, partner, sign, step, levels):
    total = partner + sign * holding
    if step == levels - 1:
        total = total * (1.0 / math.sqrt(lax.axis_size("irrep")))
    return lax.optimization_barrier(total)


def partner_of(holding, step, levels):
    owners = lax.axis_size("row")
    return exchange(holding, [owners << bit for bit in turns(step, levels)])


def in_two(value):
    high = value.astype(HALF)
    return high, (value - high.astype(jnp.float32)).astype(HALF)


def split_kernel(owners, chunks, table_ref, k_ref, high_ref, low_ref):
    depth = k_ref.shape[1] // owners // chunks
    for chunk in range(chunks):
        for piece in range(owners):
            start = (table_ref[piece] * chunks + chunk) * depth
            high, low = in_two(k_ref[:, pl.ds(pl.multiple_of(start, depth), depth)])
            at = (chunk * owners + piece) * depth
            high_ref[:, at : at + depth] = high
            low_ref[:, at : at + depth] = low


def split(table, k, chunks):
    rows, sources = k.shape
    tile = rows // 6
    block = pl.BlockSpec((tile, sources), lambda m, table: (m, 0))
    return pl.pallas_call(
        functools.partial(split_kernel, lax.axis_size("row"), chunks),
        grid_spec=pltpu.PrefetchScalarGridSpec(
            num_scalar_prefetch=1,
            grid=(rows // tile,),
            in_specs=[block],
            out_specs=[block, block],
        ),
        out_shape=[pltpu.VMEM((rows, sources), HALF)] * 2,
        cost_estimate=pl.CostEstimate(
            flops=4 * rows * sources, bytes_accessed=4 * rows * sources, transcendentals=0
        ),
        compiler_params=pltpu.CompilerParams(vmem_limit_bytes=18 * 2**20),
        name="split_reduced_kernel",
    )(table, pltpu.with_memory_space_constraint(k, pltpu.HBM))


def multiply_kernel(start, arrays, accumulate, last, high_ref, low_ref, *refs):
    refs = list(refs)
    f_refs = [refs.pop(0) for _ in range(arrays)]
    before = refs.pop(0) if accumulate else None
    out_ref, f_high, f_low = refs[:3]
    depth = f_refs[0].shape[1]
    at = 0
    for ref in f_refs:
        for piece in range(ref.shape[0]):
            high, low = in_two(ref[piece])
            f_high[at : at + depth, :] = high
            f_low[at : at + depth, :] = low
            at += depth
    sources = slice(start * depth, start * depth + at)
    tile = high_ref.shape[0] // TILES

    def product(step):
        here = pl.ds(pl.multiple_of(step * tile, tile), tile)
        high, low = high_ref[here, sources], low_ref[here, sources]
        left = jnp.concatenate([low, high, high], axis=1)
        right = jnp.concatenate([f_high[...], f_low[...], f_high[...]], axis=0)
        total = jnp.dot(left, right, preferred_element_type=jnp.float32)
        return here, total + before[here, :] if accumulate else total

    if not last:

        @pl.loop(0, TILES)
        def _(step):
            here, total = product(step)
            out_ref[here, :] = total

    else:
        result, sems = refs[3:]

        def copy(here, step):
            return pltpu.make_async_copy(
                result.at[here, :], out_ref.at[0, here, :], sems.at[step]
            )

        @pl.loop(0, TILES)
        def _(step):
            here, total = product(step)
            result[here, :] = total
            copy(here, step).start()

        for step in range(TILES):
            copy(slice(step * tile, (step + 1) * tile), step).wait()


def multiply(k_high, k_low, pieces, start, before, last=False):
    rows = k_high.shape[0]
    count, (depth, width) = sum(a.shape[0] for a in pieces), pieces[0].shape[1:]
    accumulate = before is not None
    operands = [k_high, k_low, *pieces] + ([before] if accumulate else [])
    operands = [pltpu.with_memory_space_constraint(a, pltpu.VMEM) for a in operands]
    scratch = [pltpu.VMEM((count * depth, width), HALF)] * 2
    alias = {}
    if last:
        scratch += [pltpu.VMEM((rows, width), jnp.float32), pltpu.SemaphoreType.DMA((TILES,))]
        shape = jax.ShapeDtypeStruct((1, rows, width), jnp.float32)
    else:
        shape = pltpu.VMEM((rows, width), jnp.float32)
        alias = {len(operands) - 1: 0} if accumulate else {}
    return pl.pallas_call(
        functools.partial(multiply_kernel, start, len(pieces), accumulate, last),
        in_specs=[VMEM] * len(operands),
        out_specs=ANY if last else VMEM,
        out_shape=shape,
        input_output_aliases=alias,
        scratch_shapes=scratch,
        cost_estimate=pl.CostEstimate(
            flops=int(WEIGHT * rows * count * depth * width), bytes_accessed=0, transcendentals=0
        ),
        compiler_params=pltpu.CompilerParams(vmem_limit_bytes=14 * 2**20),
        name="multiply_sources",
    )(*operands)


def after(value, others):
    return value if others is None else lax.optimization_barrier((value, others))[0]


def body(densities, reduced_kernel):
    levels = lax.axis_size("irrep").bit_length() - 1
    bits = lax.axis_size("row").bit_length() - 2
    mine = densities[0]
    half = mine.shape[0] // 2
    table, signs = numbers(levels, bits)
    ks = split(table, reduced_kernel[0], 2)
    parts = [lax.optimization_barrier(mine[at * half : (at + 1) * half]) for at in range(2)]
    for step in range(levels):
        partners = [partner_of(part, step, levels) for part in parts]
        partners[0] = after(partners[0], tuple(ks) if step == 0 else parts[1])
        parts = [fold(*pair, signs[step], step, levels) for pair in zip(parts, partners)]
    last = bits - 1
    group = lax.axis_size("row") // 2
    early = gather_chips(parts[0][None], range(last), bits)
    early = after(early, parts[1])
    arrived = across(early, last, bits)
    out = multiply(*ks, [early, exchange(early, [1, 1])], 0, None)
    late = gather_chips(parts[1][None], range(last), bits, out)
    out = multiply(*ks, [late, exchange(late, [1, 1])], 2 * group, out)
    out = multiply(*ks, [arrived, *swapped(arrived, 2)], group, out)
    arrived = after(across(late, last, bits), out)
    out = multiply(*ks, [arrived], 3 * group, out)
    return multiply(*ks, [exchange(arrived, [1, 1])], 3 * group + group // 2, out, True)


def solution(mesh):
    placed = (P("irrep", "row", None), P("irrep", "row", None))
    return jax.shard_map(
        body, mesh=mesh, in_specs=placed, out_specs=P("irrep", "row", None), check_vma=False
    )
```

```python
import functools
import itertools
import math

import jax
import jax.numpy as jnp
from jax import lax
from jax.experimental import pallas as pl
from jax.experimental.pallas import tpu as pltpu
from jax.sharding import PartitionSpec as P

HALF = jnp.bfloat16
AXES = ("irrep", "row")
TILES = (2, 4)
WEIGHT = 6


def exchange(value, masks):
    devices = lax.axis_size("irrep") * lax.axis_size("row")
    pairs = [(at, at ^ masks[at & 1]) for at in range(devices)]
    return lax.ppermute(value, AXES, pairs)


def turns(step, count):
    return [(step + core) % count for core in range(2)]


def across(held, step, bits, chunk):
    return exchange(held, [2 << bit for bit in turns(step + chunk, bits)])


def swapped(held, parts):
    size = held.shape[0] // parts
    return [exchange(held[at : at + size], [1, 1]) for at in range(0, held.shape[0], size)]


def gather_chips(held, steps, bits, chunk, others=None):
    for step in steps:
        held = jnp.concatenate([held, after(across(held, step, bits, chunk), others)])
    return held


def numbers(levels, bits):
    me = lax.axis_index("row").astype(jnp.int32)
    octant = lax.axis_index("irrep").astype(jnp.int32)
    core = me & 1
    half = 1 << (bits - 1)
    table = []
    for chunk, group, other in itertools.product(range(2), repeat=3):
        for at in range(group * half, (group + 1) * half):
            rel = [other, other]
            for step in range(bits):
                if at >> step & 1:
                    for side, bit in enumerate(turns(step + chunk, bits)):
                        rel[side] ^= 2 << bit
            table.append(me ^ jnp.where(core ^ other == 1, rel[1], rel[0]))
    signs = []
    for step in range(levels):
        bit = turns(step, levels)
        upper = octant >> jnp.where(core == 1, bit[1], bit[0]) & 1
        signs.append((1 - 2 * upper).astype(jnp.float32))
    return lax.optimization_barrier((jnp.stack(table).astype(jnp.int32), signs))


VMEM = pl.BlockSpec(memory_space=pltpu.VMEM)
SMEM = pl.BlockSpec(memory_space=pltpu.SMEM)
ANY = pl.BlockSpec(memory_space=pl.ANY)


def fold(holding, partner, sign, step, levels):
    total = partner + sign * holding
    if step == levels - 1:
        total = total * (1.0 / math.sqrt(lax.axis_size("irrep")))
    return lax.optimization_barrier(total)


def partner_of(holding, step, levels):
    owners = lax.axis_size("row")
    return exchange(holding, [owners << bit for bit in turns(step, levels)])


def in_two(value):
    high = value.astype(HALF)
    return high, (value - high.astype(jnp.float32)).astype(HALF)


def split_kernel(owners, chunks, table_ref, k_ref, high_ref, low_ref):
    depth = k_ref.shape[1] // owners // chunks
    for chunk in range(chunks):
        for piece in range(owners):
            start = (table_ref[chunk * owners + piece] * chunks + chunk) * depth
            high, low = in_two(k_ref[:, pl.ds(pl.multiple_of(start, depth), depth)])
            at = (chunk * owners + piece) * depth
            high_ref[:, at : at + depth] = high
            low_ref[:, at : at + depth] = low


def split(table, k, chunks):
    rows, sources = k.shape
    tile = rows // 8
    block = pl.BlockSpec((tile, sources), lambda m, table: (m, 0))
    return pl.pallas_call(
        functools.partial(split_kernel, lax.axis_size("row"), chunks),
        grid_spec=pltpu.PrefetchScalarGridSpec(
            num_scalar_prefetch=1,
            grid=(rows // tile,),
            in_specs=[block],
            out_specs=[block, block],
        ),
        out_shape=[pltpu.VMEM((rows, sources), HALF)] * 2,
        cost_estimate=pl.CostEstimate(
            flops=4 * rows * sources, bytes_accessed=4 * rows * sources, transcendentals=0
        ),
        compiler_params=pltpu.CompilerParams(vmem_limit_bytes=18 * 2**20),
        name="split_reduced_kernel",
    )(table, pltpu.with_memory_space_constraint(k, pltpu.HBM))


def multiply_kernel(start, arrays, accumulate, last, high_ref, low_ref, *refs):
    refs = list(refs)
    f_refs = [refs.pop(0) for _ in range(arrays)]
    before = refs.pop(0) if accumulate else None
    out_ref, f_high, f_low = refs[:3]
    depth = f_refs[0].shape[1]
    at = 0
    for ref in f_refs:
        for piece in range(ref.shape[0]):
            high, low = in_two(ref[piece])
            f_high[at : at + depth, :] = high
            f_low[at : at + depth, :] = low
            at += depth
    sources = slice(start * depth, start * depth + at)
    tiles = TILES[last]
    tile = high_ref.shape[0] // tiles

    def product(step):
        here = pl.ds(pl.multiple_of(step * tile, tile), tile)
        high, low = high_ref[here, sources], low_ref[here, sources]
        left = jnp.concatenate([low, high, high], axis=1)
        right = jnp.concatenate([f_high[...], f_low[...], f_high[...]], axis=0)
        total = jnp.dot(left, right, preferred_element_type=jnp.float32)
        return here, total + before[here, :] if accumulate else total

    if not last:

        @pl.loop(0, tiles)
        def _(step):
            here, total = product(step)
            out_ref[here, :] = total

    else:
        result, sems = refs[3:]

        def copy(here, step):
            return pltpu.make_async_copy(
                result.at[here, :], out_ref.at[0, here, :], sems.at[step]
            )

        @pl.loop(0, tiles)
        def _(step):
            here, total = product(step)
            result[here, :] = total
            copy(here, step).start()

        for step in range(tiles):
            copy(slice(step * tile, (step + 1) * tile), step).wait()


def multiply(k_high, k_low, pieces, start, before, last=False):
    rows = k_high.shape[0]
    count, (depth, width) = sum(a.shape[0] for a in pieces), pieces[0].shape[1:]
    accumulate = before is not None
    operands = [k_high, k_low, *pieces] + ([before] if accumulate else [])
    operands = [pltpu.with_memory_space_constraint(a, pltpu.VMEM) for a in operands]
    scratch = [pltpu.VMEM((count * depth, width), HALF)] * 2
    alias = {}
    if last:
        scratch += [pltpu.VMEM((rows, width), jnp.float32), pltpu.SemaphoreType.DMA((TILES[1],))]
        shape = jax.ShapeDtypeStruct((1, rows, width), jnp.float32)
    else:
        shape = pltpu.VMEM((rows, width), jnp.float32)
        alias = {len(operands) - 1: 0} if accumulate else {}
    return pl.pallas_call(
        functools.partial(multiply_kernel, start, len(pieces), accumulate, last),
        in_specs=[VMEM] * len(operands),
        out_specs=ANY if last else VMEM,
        out_shape=shape,
        input_output_aliases=alias,
        scratch_shapes=scratch,
        cost_estimate=pl.CostEstimate(
            flops=int(WEIGHT * rows * count * depth * width), bytes_accessed=0, transcendentals=0
        ),
        compiler_params=pltpu.CompilerParams(vmem_limit_bytes=14 * 2**20),
        name="multiply_sources",
    )(*operands)


def after(value, others):
    return value if others is None else lax.optimization_barrier((value, others))[0]


def body(densities, reduced_kernel):
    levels = lax.axis_size("irrep").bit_length() - 1
    bits = lax.axis_size("row").bit_length() - 2
    mine = densities[0]
    half = mine.shape[0] // 2
    table, signs = numbers(levels, bits)
    ks = split(table, reduced_kernel[0], 2)
    parts = [lax.optimization_barrier(mine[at * half : (at + 1) * half]) for at in range(2)]
    for step in range(levels):
        partners = [partner_of(part, step, levels) for part in parts]
        partners[0] = after(partners[0], tuple(ks) if step == 0 else parts[1])
        parts = [fold(*pair, signs[step], step, levels) for pair in zip(parts, partners)]
    last = bits - 1
    group = lax.axis_size("row") // 2
    early = gather_chips(parts[0][None], range(last), bits, 0)
    early = after(early, parts[1])
    arrived = across(early, last, bits, 0)
    out = multiply(*ks, [early, exchange(early, [1, 1])], 0, None)
    late = gather_chips(parts[1][None], range(last), bits, 1, out)
    out = multiply(*ks, [late, exchange(late, [1, 1])], 2 * group, out)
    out = multiply(*ks, [arrived, *swapped(arrived, 2)], group, out)
    arrived = after(across(late, last, bits, 1), out)
    out = multiply(*ks, [arrived], 3 * group, out)
    return multiply(*ks, [exchange(arrived, [1, 1])], 3 * group + group // 2, out, True)


def solution(mesh):
    placed = (P("irrep", "row", None), P("irrep", "row", None))
    return jax.shard_map(
        body, mesh=mesh, in_specs=placed, out_specs=P("irrep", "row", None), check_vma=False
    )
```

```python
import functools
import itertools
import math

import jax
import jax.numpy as jnp
from jax import lax
from jax.experimental import pallas as pl
from jax.experimental.pallas import tpu as pltpu
from jax.sharding import PartitionSpec as P

HALF = jnp.bfloat16
AXES = ("irrep", "row")
TILES = (2, 2)


def exchange(value, masks):
    devices = lax.axis_size("irrep") * lax.axis_size("row")
    pairs = [(at, at ^ masks[at & 1]) for at in range(devices)]
    return lax.ppermute(value, AXES, pairs)


def turns(step, count):
    return [(step + core) % count for core in range(2)]


def across(held, step, bits):
    return exchange(held, [2 << bit for bit in turns(step, bits)])


def swapped(held, parts):
    size = held.shape[0] // parts
    return [exchange(held[at : at + size], [1, 1]) for at in range(0, held.shape[0], size)]


def numbers(levels, bits):
    me = lax.axis_index("row").astype(jnp.int32)
    octant = lax.axis_index("irrep").astype(jnp.int32)
    core = me & 1
    table = []
    for stage, other in itertools.product(range(bits + 1), range(2)):
        for at in range(1 << stage >> 1, 1 << stage):
            rel = [other, other]
            for step in range(bits):
                if at >> step & 1:
                    for side, bit in enumerate(turns(step, bits)):
                        rel[side] ^= 2 << bit
            table.append(me ^ jnp.where(core ^ other == 1, rel[1], rel[0]))
    signs = []
    for step in range(levels):
        bit = turns(step, levels)
        upper = octant >> jnp.where(core == 1, bit[1], bit[0]) & 1
        signs.append((1 - 2 * upper).astype(jnp.float32))
    return lax.optimization_barrier((jnp.stack(table).astype(jnp.int32), signs))


VMEM = pl.BlockSpec(memory_space=pltpu.VMEM)
SMEM = pl.BlockSpec(memory_space=pltpu.SMEM)
ANY = pl.BlockSpec(memory_space=pl.ANY)


def fold(holding, partner, sign, step, levels):
    total = partner + sign * holding
    if step == levels - 1:
        total = total * (1.0 / math.sqrt(lax.axis_size("irrep")))
    return total


def partner_of(holding, step, levels):
    owners = lax.axis_size("row")
    return exchange(holding, [owners << bit for bit in turns(step, levels)])


def in_two(value):
    high = value.astype(HALF)
    return high, (value - high.astype(jnp.float32)).astype(HALF)


def split_kernel(owners, chunks, table_ref, k_ref, high_ref, low_ref):
    depth = k_ref.shape[1] // owners // chunks
    for chunk in range(chunks):
        for piece in range(owners):
            start = (table_ref[piece] * chunks + chunk) * depth
            high, low = in_two(k_ref[:, pl.ds(pl.multiple_of(start, depth), depth)])
            at = (chunk * owners + piece) * depth
            high_ref[:, at : at + depth] = high
            low_ref[:, at : at + depth] = low


def split(table, k, chunks):
    rows, sources = k.shape
    tile = rows // 8
    block = pl.BlockSpec((tile, sources), lambda m, table: (m, 0))
    return pl.pallas_call(
        functools.partial(split_kernel, lax.axis_size("row"), chunks),
        grid_spec=pltpu.PrefetchScalarGridSpec(
            num_scalar_prefetch=1,
            grid=(rows // tile,),
            in_specs=[block],
            out_specs=[block, block],
        ),
        out_shape=[pltpu.VMEM((rows, sources), HALF)] * 2,
        cost_estimate=pl.CostEstimate(
            flops=4 * rows * sources, bytes_accessed=4 * rows * sources, transcendentals=0
        ),
        compiler_params=pltpu.CompilerParams(vmem_limit_bytes=18 * 2**20),
        name="split_reduced_kernel",
    )(table, pltpu.with_memory_space_constraint(k, pltpu.HBM))


def multiply_kernel(start, arrays, accumulate, last, high_ref, low_ref, *refs):
    refs = list(refs)
    f_refs = [[refs.pop(0) for _ in range(count)] for count in arrays]
    before = refs.pop(0) if accumulate else None
    out_ref, f_high, f_low = refs[:3]
    depth, width = f_refs[0][0].shape[1:]
    for part, of in enumerate(f_refs):
        columns = slice(part * width, (part + 1) * width)
        at = 0
        for ref in of:
            for piece in range(ref.shape[0]):
                high, low = in_two(ref[piece])
                f_high[at : at + depth, columns] = high
                f_low[at : at + depth, columns] = low
                at += depth
    sources = slice(start * depth, start * depth + at)
    tiles = TILES[last]
    tile = high_ref.shape[0] // tiles

    def product(step):
        here = pl.ds(pl.multiple_of(step * tile, tile), tile)
        high, low = high_ref[here, sources], low_ref[here, sources]
        left = jnp.concatenate([low, high, high], axis=1)
        right = jnp.concatenate([f_high[...], f_low[...], f_high[...]], axis=0)
        total = jnp.dot(left, right, preferred_element_type=jnp.float32)
        return here, total + before[here, :] if accumulate else total

    if not last:

        @pl.loop(0, tiles)
        def _(step):
            here, total = product(step)
            out_ref[here, :] = total

    else:
        result, sems = refs[3:]

        def copy(here, step):
            return pltpu.make_async_copy(
                result.at[here, :], out_ref.at[0, here, :], sems.at[step]
            )

        @pl.loop(0, tiles)
        def _(step):
            here, total = product(step)
            result[here, :] = total
            copy(here, step).start()

        for step in range(tiles):
            copy(slice(step * tile, (step + 1) * tile), step).wait()


def multiply(k_high, k_low, pieces, start, before, last=False, weight=6):
    rows, (depth, width) = k_high.shape[0], pieces[0][0].shape[1:]
    count, width = sum(a.shape[0] for a in pieces[0]), width * len(pieces)
    accumulate = before is not None
    operands = [k_high, k_low, *itertools.chain(*pieces)] + ([before] if accumulate else [])
    operands = [pltpu.with_memory_space_constraint(a, pltpu.VMEM) for a in operands]
    scratch = [pltpu.VMEM((count * depth, width), HALF)] * 2
    alias = {}
    if last:
        scratch += [pltpu.VMEM((rows, width), jnp.float32), pltpu.SemaphoreType.DMA((TILES[1],))]
        shape = jax.ShapeDtypeStruct((1, rows, width), jnp.float32)
    else:
        shape = pltpu.VMEM((rows, width), jnp.float32)
        alias = {len(operands) - 1: 0} if accumulate else {}
    return pl.pallas_call(
        functools.partial(multiply_kernel, start, [len(of) for of in pieces], accumulate, last),
        in_specs=[VMEM] * len(operands),
        out_specs=ANY if last else VMEM,
        out_shape=shape,
        input_output_aliases=alias,
        scratch_shapes=scratch,
        cost_estimate=pl.CostEstimate(
            flops=int(weight * rows * count * depth * width), bytes_accessed=0, transcendentals=0
        ),
        compiler_params=pltpu.CompilerParams(vmem_limit_bytes=14 * 2**20),
        name="multiply_sources",
    )(*operands)


def after(value, others):
    return value if others is None else lax.optimization_barrier((value, others))[0]


def body(densities, reduced_kernel):
    levels = lax.axis_size("irrep").bit_length() - 1
    bits = lax.axis_size("row").bit_length() - 2
    mine = densities[0]
    half = mine.shape[0] // 2
    table, signs = numbers(levels, bits)
    ks = split(table, reduced_kernel[0], 2)
    early, late = mine[:half], mine[half:]
    owners = lax.axis_size("row")
    for step in range(levels):
        early, late = [lax.optimization_barrier(part) for part in (early, late)]
        partners = [partner_of(part, step, levels) for part in (early, late)]
        partners[0] = after(partners[0], tuple(ks) if step == 0 else late)
        early = fold(early, partners[0], signs[step], step, levels)
        late = fold(late, partners[1], signs[step], step, levels)
    early, late = [lax.optimization_barrier(part[None]) for part in (early, late)]
    pieces, others = [early], [*swapped(early, 1)]
    for step in range(bits - 1):
        pieces.append(across(early, step, bits))
        others += swapped(pieces[-1], 1)
        early = jnp.concatenate([early, pieces[-1]])
    early = after(early, late)
    first = across(early, bits - 1, bits)
    pieces = [*itertools.chain(*zip(pieces, others))]
    out = multiply(*ks, [pieces], 0, None)
    out = multiply(*ks, [[late, *swapped(late, 1)]], owners, out, weight=0)
    for step in range(bits - 1):
        second = after(across(late, step, bits), out)
        out = multiply(*ks, [[second, *swapped(second, 1)]], owners + (2 << step), out)
        late = jnp.concatenate([late, second])
    out = multiply(*ks, [[first, *swapped(first, 2)]], 1 << bits, out)
    second = after(across(late, bits - 1, bits), out)
    start = owners + (1 << bits)
    out = multiply(*ks, [[second]], start, out)
    return multiply(*ks, [swapped(second, 1)], start + second.shape[0], out, True)


def solution(mesh):
    placed = (P("irrep", "row", None), P("irrep", "row", None))
    return jax.shard_map(
        body, mesh=mesh, in_specs=placed, out_specs=P("irrep", "row", None), check_vma=False
    )
```

```python
import functools
import itertools
import math

import jax
import jax.numpy as jnp
from jax import lax
from jax.experimental import pallas as pl
from jax.experimental.pallas import tpu as pltpu
from jax.sharding import PartitionSpec as P

HALF = jnp.bfloat16
AXES = ("irrep", "row")
TILES = (2, 2)


def exchange(value, masks):
    devices = lax.axis_size("irrep") * lax.axis_size("row")
    pairs = [(at, at ^ masks[at & 1]) for at in range(devices)]
    return lax.ppermute(value, AXES, pairs)


def turns(step, count):
    return [(step + core) % count for core in range(2)]


def across(held, step, bits):
    return exchange(held, [2 << bit for bit in turns(step, bits)])


def swapped(held, parts):
    size = held.shape[0] // parts
    return [exchange(held[at : at + size], [1, 1]) for at in range(0, held.shape[0], size)]


def numbers(levels, bits):
    me = lax.axis_index("row").astype(jnp.int32)
    octant = lax.axis_index("irrep").astype(jnp.int32)
    core = me & 1
    table = []
    for stage, other in itertools.product(range(bits + 1), range(2)):
        for at in range(1 << stage >> 1, 1 << stage):
            rel = [other, other]
            for step in range(bits):
                if at >> step & 1:
                    for side, bit in enumerate(turns(step, bits)):
                        rel[side] ^= 2 << bit
            table.append(me ^ jnp.where(core ^ other == 1, rel[1], rel[0]))
    signs = []
    for step in range(levels):
        bit = turns(step, levels)
        upper = octant >> jnp.where(core == 1, bit[1], bit[0]) & 1
        signs.append((1 - 2 * upper).astype(jnp.float32))
    return lax.optimization_barrier((jnp.stack(table).astype(jnp.int32), signs))


VMEM = pl.BlockSpec(memory_space=pltpu.VMEM)
SMEM = pl.BlockSpec(memory_space=pltpu.SMEM)
ANY = pl.BlockSpec(memory_space=pl.ANY)


def fold(holding, partner, sign, step, levels):
    total = partner + sign * holding
    if step == levels - 1:
        total = total * (1.0 / math.sqrt(lax.axis_size("irrep")))
    return total


def partner_of(holding, step, levels):
    owners = lax.axis_size("row")
    return exchange(holding, [owners << bit for bit in turns(step, levels)])


def in_two(value):
    high = value.astype(HALF)
    return high, (value - high.astype(jnp.float32)).astype(HALF)


def split_kernel(owners, chunks, table_ref, k_ref, high_ref, low_ref):
    depth = k_ref.shape[1] // owners // chunks
    for chunk in range(chunks):
        for piece in range(owners):
            start = (table_ref[piece] * chunks + chunk) * depth
            high, low = in_two(k_ref[:, pl.ds(pl.multiple_of(start, depth), depth)])
            at = (chunk * owners + piece) * depth
            high_ref[:, at : at + depth] = high
            low_ref[:, at : at + depth] = low


def split(table, k, chunks):
    rows, sources = k.shape
    tile = rows // 8
    block = pl.BlockSpec((tile, sources), lambda m, table: (m, 0))
    return pl.pallas_call(
        functools.partial(split_kernel, lax.axis_size("row"), chunks),
        grid_spec=pltpu.PrefetchScalarGridSpec(
            num_scalar_prefetch=1,
            grid=(rows // tile,),
            in_specs=[block],
            out_specs=[block, block],
        ),
        out_shape=[pltpu.VMEM((rows, sources), HALF)] * 2,
        cost_estimate=pl.CostEstimate(
            flops=4 * rows * sources, bytes_accessed=4 * rows * sources, transcendentals=0
        ),
        compiler_params=pltpu.CompilerParams(vmem_limit_bytes=18 * 2**20),
        name="split_reduced_kernel",
    )(table, pltpu.with_memory_space_constraint(k, pltpu.HBM))


def multiply_kernel(start, arrays, accumulate, last, high_ref, low_ref, *refs):
    refs = list(refs)
    f_refs = [[refs.pop(0) for _ in range(count)] for count in arrays]
    before = refs.pop(0) if accumulate else None
    out_ref, f_high, f_low = refs[:3]
    depth, width = f_refs[0][0].shape[1:]
    for part, of in enumerate(f_refs):
        columns = slice(part * width, (part + 1) * width)
        at = 0
        for ref in of:
            for piece in range(ref.shape[0]):
                high, low = in_two(ref[piece])
                f_high[at : at + depth, columns] = high
                f_low[at : at + depth, columns] = low
                at += depth
    sources = slice(start * depth, start * depth + at)
    tiles = TILES[last]
    tile = high_ref.shape[0] // tiles

    def product(step):
        here = pl.ds(pl.multiple_of(step * tile, tile), tile)
        high, low = high_ref[here, sources], low_ref[here, sources]
        left = jnp.concatenate([low, high, high], axis=1)
        right = jnp.concatenate([f_high[...], f_low[...], f_high[...]], axis=0)
        total = jnp.dot(left, right, preferred_element_type=jnp.float32)
        return here, total + before[here, :] if accumulate else total

    if not last:

        @pl.loop(0, tiles)
        def _(step):
            here, total = product(step)
            out_ref[here, :] = total

    else:
        result, sems = refs[3:]

        def copy(here, step):
            return pltpu.make_async_copy(
                result.at[here, :], out_ref.at[0, here, :], sems.at[step]
            )

        @pl.loop(0, tiles)
        def _(step):
            here, total = product(step)
            result[here, :] = total
            copy(here, step).start()

        for step in range(tiles):
            copy(slice(step * tile, (step + 1) * tile), step).wait()


def multiply(k_high, k_low, pieces, start, before, last=False, weight=6):
    rows, (depth, width) = k_high.shape[0], pieces[0][0].shape[1:]
    count, width = sum(a.shape[0] for a in pieces[0]), width * len(pieces)
    accumulate = before is not None
    operands = [k_high, k_low, *itertools.chain(*pieces)] + ([before] if accumulate else [])
    operands = [pltpu.with_memory_space_constraint(a, pltpu.VMEM) for a in operands]
    scratch = [pltpu.VMEM((count * depth, width), HALF)] * 2
    alias = {}
    if last:
        scratch += [pltpu.VMEM((rows, width), jnp.float32), pltpu.SemaphoreType.DMA((TILES[1],))]
        shape = jax.ShapeDtypeStruct((1, rows, width), jnp.float32)
    else:
        shape = pltpu.VMEM((rows, width), jnp.float32)
        alias = {len(operands) - 1: 0} if accumulate else {}
    return pl.pallas_call(
        functools.partial(multiply_kernel, start, [len(of) for of in pieces], accumulate, last),
        in_specs=[VMEM] * len(operands),
        out_specs=ANY if last else VMEM,
        out_shape=shape,
        input_output_aliases=alias,
        scratch_shapes=scratch,
        cost_estimate=pl.CostEstimate(
            flops=int(weight * rows * count * depth * width), bytes_accessed=0, transcendentals=0
        ),
        compiler_params=pltpu.CompilerParams(vmem_limit_bytes=14 * 2**20),
        name="multiply_sources",
    )(*operands)


def after(value, others):
    return value if others is None else lax.optimization_barrier((value, others))[0]


def body(densities, reduced_kernel):
    levels = lax.axis_size("irrep").bit_length() - 1
    bits = lax.axis_size("row").bit_length() - 2
    mine = densities[0]
    half = mine.shape[0] // 2
    table, signs = numbers(levels, bits)
    ks = split(table, reduced_kernel[0], 2)
    early, late = mine[:half], mine[half:]
    owners = lax.axis_size("row")
    for step in range(levels):
        early, late = [lax.optimization_barrier(part) for part in (early, late)]
        partners = [partner_of(part, step, levels) for part in (early, late)]
        partners[0] = after(partners[0], tuple(ks) if step == 0 else late)
        early = fold(early, partners[0], signs[step], step, levels)
        late = fold(late, partners[1], signs[step], step, levels)
    early, late = [lax.optimization_barrier(part[None]) for part in (early, late)]
    pieces, others = [early], [*swapped(early, 1)]
    for step in range(bits - 1):
        pieces.append(after(across(early, step, bits), late))
        others += swapped(pieces[-1], 1)
        early = jnp.concatenate([early, pieces[-1]])
    first = across(early, bits - 1, bits)
    pieces = [*itertools.chain(*zip(pieces, others))]
    out = multiply(*ks, [pieces], 0, None, weight=12)
    out = multiply(*ks, [[late, *swapped(late, 1)]], owners, out, weight=0)
    for step in range(bits - 1):
        second = after(across(late, step, bits), out)
        out = multiply(*ks, [[second, *swapped(second, 1)]], owners + (2 << step), out)
        late = jnp.concatenate([late, second])
    out = multiply(*ks, [[first, *swapped(first, 2)]], 1 << bits, out)
    second = after(across(late, bits - 1, bits), out)
    start = owners + (1 << bits)
    out = multiply(*ks, [[second]], start, out)
    return multiply(*ks, [swapped(second, 1)], start + second.shape[0], out, True)


def solution(mesh):
    placed = (P("irrep", "row", None), P("irrep", "row", None))
    return jax.shard_map(
        body, mesh=mesh, in_specs=placed, out_specs=P("irrep", "row", None), check_vma=False
    )
```

```python
import functools
import itertools
import math

import jax
import jax.numpy as jnp
from jax import lax
from jax.experimental import pallas as pl
from jax.experimental.pallas import tpu as pltpu
from jax.sharding import PartitionSpec as P

HALF = jnp.bfloat16
AXES = ("irrep", "row")
TILES = (2, 3)
COPIES = 4


def exchange(value, masks):
    devices = lax.axis_size("irrep") * lax.axis_size("row")
    pairs = [(at, at ^ masks[at & 1]) for at in range(devices)]
    return lax.ppermute(value, AXES, pairs)


def turns(step, count):
    return [(step + core) % count for core in range(2)]


def across(held, step, bits):
    return exchange(held, [2 << bit for bit in turns(step, bits)])


def swapped(held, parts):
    size = held.shape[0] // parts
    return [exchange(held[at : at + size], [1, 1]) for at in range(0, held.shape[0], size)]


def numbers(levels, bits):
    me = lax.axis_index("row").astype(jnp.int32)
    octant = lax.axis_index("irrep").astype(jnp.int32)
    core = me & 1
    table = []
    for stage, other in itertools.product(range(bits + 1), range(2)):
        for at in range(1 << stage >> 1, 1 << stage):
            rel = [other, other]
            for step in range(bits):
                if at >> step & 1:
                    for side, bit in enumerate(turns(step, bits)):
                        rel[side] ^= 2 << bit
            table.append(me ^ jnp.where(core ^ other == 1, rel[1], rel[0]))
    signs = []
    for step in range(levels):
        bit = turns(step, levels)
        upper = octant >> jnp.where(core == 1, bit[1], bit[0]) & 1
        signs.append((1 - 2 * upper).astype(jnp.float32))
    return lax.optimization_barrier((jnp.stack(table).astype(jnp.int32), signs))


VMEM = pl.BlockSpec(memory_space=pltpu.VMEM)
SMEM = pl.BlockSpec(memory_space=pltpu.SMEM)
ANY = pl.BlockSpec(memory_space=pl.ANY)


def fold(holding, partner, sign, step, levels):
    total = partner + sign * holding
    if step == levels - 1:
        total = total * (1.0 / math.sqrt(lax.axis_size("irrep")))
    return total


def partner_of(holding, step, levels):
    owners = lax.axis_size("row")
    return exchange(holding, [owners << bit for bit in turns(step, levels)])


def in_two(value):
    high = value.astype(HALF)
    return high, (value - high.astype(jnp.float32)).astype(HALF)


def split_kernel(owners, chunks, table_ref, k_ref, high_ref, low_ref):
    depth = k_ref.shape[1] // owners // chunks
    for chunk in range(chunks):
        for piece in range(owners):
            start = (table_ref[piece] * chunks + chunk) * depth
            high, low = in_two(k_ref[:, pl.ds(pl.multiple_of(start, depth), depth)])
            at = (chunk * owners + piece) * depth
            high_ref[:, at : at + depth] = high
            low_ref[:, at : at + depth] = low


def split(table, k, chunks):
    rows, sources = k.shape
    tile = rows // 8
    block = pl.BlockSpec((tile, sources), lambda m, table: (m, 0))
    return pl.pallas_call(
        functools.partial(split_kernel, lax.axis_size("row"), chunks),
        grid_spec=pltpu.PrefetchScalarGridSpec(
            num_scalar_prefetch=1,
            grid=(rows // tile,),
            in_specs=[block],
            out_specs=[block, block],
        ),
        out_shape=[pltpu.VMEM((rows, sources), HALF)] * 2,
        cost_estimate=pl.CostEstimate(
            flops=4 * rows * sources, bytes_accessed=4 * rows * sources, transcendentals=0
        ),
        compiler_params=pltpu.CompilerParams(vmem_limit_bytes=18 * 2**20),
        name="split_reduced_kernel",
    )(table, pltpu.with_memory_space_constraint(k, pltpu.HBM))


def multiply_kernel(start, arrays, accumulate, last, high_ref, low_ref, *refs):
    refs = list(refs)
    f_refs = [[refs.pop(0) for _ in range(count)] for count in arrays]
    before = refs.pop(0) if accumulate else None
    out_ref, f_high, f_low = refs[:3]
    depth, width = f_refs[0][0].shape[1:]
    for part, of in enumerate(f_refs):
        columns = slice(part * width, (part + 1) * width)
        at = 0
        for ref in of:
            for piece in range(ref.shape[0]):
                high, low = in_two(ref[piece])
                f_high[at : at + depth, columns] = high
                f_low[at : at + depth, columns] = low
                at += depth
    sources = slice(start * depth, start * depth + at)
    tiles = TILES[last]
    tile = high_ref.shape[0] // tiles

    def product(step):
        here = pl.ds(pl.multiple_of(step * tile, tile), tile)
        high, low = high_ref[here, sources], low_ref[here, sources]
        left = jnp.concatenate([low, high, high], axis=1)
        right = jnp.concatenate([f_high[...], f_low[...], f_high[...]], axis=0)
        total = jnp.dot(left, right, preferred_element_type=jnp.float32)
        return here, total + before[here, :] if accumulate else total

    if not last:

        @pl.loop(0, tiles)
        def _(step):
            here, total = product(step)
            out_ref[here, :] = total

    else:
        result, sems = refs[3:]

        size = tile // COPIES

        def copy(number):
            here = pl.ds(pl.multiple_of(number * size, size), size)
            return pltpu.make_async_copy(
                result.at[here, :], out_ref.at[0, here, :], sems.at[number]
            )

        @pl.loop(0, tiles)
        def _(step):
            here, total = product(step)
            result[here, :] = total
            for part in range(COPIES):
                number = step * COPIES + part
                copy(number).start()

        for number in range(tiles * COPIES):
            copy(number).wait()


def multiply(k_high, k_low, pieces, start, before, last=False, weight=6):
    rows, (depth, width) = k_high.shape[0], pieces[0][0].shape[1:]
    count, width = sum(a.shape[0] for a in pieces[0]), width * len(pieces)
    accumulate = before is not None
    operands = [k_high, k_low, *itertools.chain(*pieces)] + ([before] if accumulate else [])
    operands = [pltpu.with_memory_space_constraint(a, pltpu.VMEM) for a in operands]
    scratch = [pltpu.VMEM((count * depth, width), HALF)] * 2
    alias = {}
    if last:
        scratch += [pltpu.VMEM((rows, width), jnp.float32), pltpu.SemaphoreType.DMA((TILES[1] * COPIES,))]
        shape = jax.ShapeDtypeStruct((1, rows, width), jnp.float32)
    else:
        shape = pltpu.VMEM((rows, width), jnp.float32)
        alias = {len(operands) - 1: 0} if accumulate else {}
    return pl.pallas_call(
        functools.partial(multiply_kernel, start, [len(of) for of in pieces], accumulate, last),
        in_specs=[VMEM] * len(operands),
        out_specs=ANY if last else VMEM,
        out_shape=shape,
        input_output_aliases=alias,
        scratch_shapes=scratch,
        cost_estimate=pl.CostEstimate(
            flops=int(weight * rows * count * depth * width), bytes_accessed=0, transcendentals=0
        ),
        compiler_params=pltpu.CompilerParams(vmem_limit_bytes=14 * 2**20),
        name="multiply_sources",
    )(*operands)


def after(value, others):
    return value if others is None else lax.optimization_barrier((value, others))[0]


def body(densities, reduced_kernel):
    levels = lax.axis_size("irrep").bit_length() - 1
    bits = lax.axis_size("row").bit_length() - 2
    mine = densities[0]
    half = mine.shape[0] // 2
    table, signs = numbers(levels, bits)
    ks = split(table, reduced_kernel[0], 2)
    early, late = mine[:half], mine[half:]
    owners = lax.axis_size("row")
    for step in range(levels):
        early, late = [lax.optimization_barrier(part) for part in (early, late)]
        partners = [partner_of(part, step, levels) for part in (early, late)]
        partners[0] = after(partners[0], tuple(ks) if step == 0 else late)
        early = fold(early, partners[0], signs[step], step, levels)
        late = fold(late, partners[1], signs[step], step, levels)
    early, late = [lax.optimization_barrier(part[None]) for part in (early, late)]
    pieces, others = [early], [*swapped(early, 1)]
    for step in range(bits - 1):
        pieces.append(after(across(early, step, bits), late))
        others += swapped(pieces[-1], 1)
        early = jnp.concatenate([early, pieces[-1]])
    first = across(early, bits - 1, bits)
    pieces = [*itertools.chain(*zip(pieces, others))]
    out = multiply(*ks, [pieces], 0, None, weight=12)
    out = multiply(*ks, [[late, *swapped(late, 1)]], owners, out, weight=0)
    for step in range(bits - 1):
        second = after(across(late, step, bits), out)
        out = multiply(*ks, [[second, *swapped(second, 1)]], owners + (2 << step), out)
        late = jnp.concatenate([late, second])
    out = multiply(*ks, [[first, *swapped(first, 2)]], 1 << bits, out)
    second = after(across(late, bits - 1, bits), out)
    start = owners + (1 << bits)
    out = multiply(*ks, [[second]], start, out)
    return multiply(*ks, [swapped(second, 1)], start + second.shape[0], out, True)


def solution(mesh):
    placed = (P("irrep", "row", None), P("irrep", "row", None))
    return jax.shard_map(
        body, mesh=mesh, in_specs=placed, out_specs=P("irrep", "row", None), check_vma=False
    )
```

```python
import functools
import itertools
import math

import jax
import jax.numpy as jnp
from jax import lax
from jax.experimental import pallas as pl
from jax.experimental.pallas import tpu as pltpu
from jax.sharding import PartitionSpec as P

HALF = jnp.bfloat16
AXES = ("irrep", "row")
TILES = (2, 3)
COPIES = 4


def exchange(value, masks):
    devices = lax.axis_size("irrep") * lax.axis_size("row")
    pairs = [(at, at ^ masks[at & 1]) for at in range(devices)]
    return lax.ppermute(value, AXES, pairs)


def turns(step, count):
    return [(step + core) % count for core in range(2)]


def across(held, step, bits, chunk):
    return exchange(held, [2 << bit for bit in turns(step + chunk, bits)])


def swapped(held, parts):
    size = held.shape[0] // parts
    return [exchange(held[at : at + size], [1, 1]) for at in range(0, held.shape[0], size)]


def numbers(levels, bits):
    me = lax.axis_index("row").astype(jnp.int32)
    octant = lax.axis_index("irrep").astype(jnp.int32)
    core = me & 1
    table = []
    for chunk, stage, other in itertools.product(range(2), range(bits + 1), range(2)):
        for at in range(1 << stage >> 1, 1 << stage):
            rel = [other, other]
            for step in range(bits):
                if at >> step & 1:
                    for side, bit in enumerate(turns(step + chunk, bits)):
                        rel[side] ^= 2 << bit
            table.append(me ^ jnp.where(core ^ other == 1, rel[1], rel[0]))
    signs = []
    for step in range(levels):
        bit = turns(step, levels)
        upper = octant >> jnp.where(core == 1, bit[1], bit[0]) & 1
        signs.append((1 - 2 * upper).astype(jnp.float32))
    return lax.optimization_barrier((jnp.stack(table).astype(jnp.int32), signs))


VMEM = pl.BlockSpec(memory_space=pltpu.VMEM)
SMEM = pl.BlockSpec(memory_space=pltpu.SMEM)
ANY = pl.BlockSpec(memory_space=pl.ANY)


def fold(holding, partner, sign, step, levels):
    total = partner + sign * holding
    if step == levels - 1:
        total = total * (1.0 / math.sqrt(lax.axis_size("irrep")))
    return total


def partner_of(holding, step, levels):
    owners = lax.axis_size("row")
    return exchange(holding, [owners << bit for bit in turns(step, levels)])


def in_two(value):
    high = value.astype(HALF)
    return high, (value - high.astype(jnp.float32)).astype(HALF)


def split_kernel(owners, chunks, table_ref, k_ref, high_ref, low_ref):
    depth = k_ref.shape[1] // owners // chunks
    for chunk in range(chunks):
        for piece in range(owners):
            start = (table_ref[chunk * owners + piece] * chunks + chunk) * depth
            high, low = in_two(k_ref[:, pl.ds(pl.multiple_of(start, depth), depth)])
            at = (chunk * owners + piece) * depth
            high_ref[:, at : at + depth] = high
            low_ref[:, at : at + depth] = low


def split(table, k, chunks):
    rows, sources = k.shape
    tile = rows // 8
    block = pl.BlockSpec((tile, sources), lambda m, table: (m, 0))
    return pl.pallas_call(
        functools.partial(split_kernel, lax.axis_size("row"), chunks),
        grid_spec=pltpu.PrefetchScalarGridSpec(
            num_scalar_prefetch=1,
            grid=(rows // tile,),
            in_specs=[block],
            out_specs=[block, block],
        ),
        out_shape=[pltpu.VMEM((rows, sources), HALF)] * 2,
        cost_estimate=pl.CostEstimate(
            flops=4 * rows * sources, bytes_accessed=4 * rows * sources, transcendentals=0
        ),
        compiler_params=pltpu.CompilerParams(vmem_limit_bytes=18 * 2**20),
        name="split_reduced_kernel",
    )(table, pltpu.with_memory_space_constraint(k, pltpu.HBM))


def multiply_kernel(start, arrays, accumulate, last, high_ref, low_ref, *refs):
    refs = list(refs)
    f_refs = [[refs.pop(0) for _ in range(count)] for count in arrays]
    before = refs.pop(0) if accumulate else None
    out_ref, f_high, f_low = refs[:3]
    depth, width = f_refs[0][0].shape[1:]
    for part, of in enumerate(f_refs):
        columns = slice(part * width, (part + 1) * width)
        at = 0
        for ref in of:
            for piece in range(ref.shape[0]):
                high, low = in_two(ref[piece])
                f_high[at : at + depth, columns] = high
                f_low[at : at + depth, columns] = low
                at += depth
    sources = slice(start * depth, start * depth + at)
    tiles = TILES[last]
    tile = high_ref.shape[0] // tiles

    def product(step):
        here = pl.ds(pl.multiple_of(step * tile, tile), tile)
        high, low = high_ref[here, sources], low_ref[here, sources]
        left = jnp.concatenate([low, high, high], axis=1)
        right = jnp.concatenate([f_high[...], f_low[...], f_high[...]], axis=0)
        total = jnp.dot(left, right, preferred_element_type=jnp.float32)
        return here, total + before[here, :] if accumulate else total

    if not last:

        @pl.loop(0, tiles)
        def _(step):
            here, total = product(step)
            out_ref[here, :] = total

    else:
        result, sems = refs[3:]

        size = tile // COPIES

        def copy(number):
            here = pl.ds(pl.multiple_of(number * size, size), size)
            return pltpu.make_async_copy(
                result.at[here, :], out_ref.at[0, here, :], sems.at[number]
            )

        @pl.loop(0, tiles)
        def _(step):
            here, total = product(step)
            result[here, :] = total
            for part in range(COPIES):
                number = step * COPIES + part
                copy(number).start()

        for number in range(tiles * COPIES):
            copy(number).wait()


def multiply(k_high, k_low, pieces, start, before, last=False, weight=6):
    rows, (depth, width) = k_high.shape[0], pieces[0][0].shape[1:]
    count, width = sum(a.shape[0] for a in pieces[0]), width * len(pieces)
    accumulate = before is not None
    operands = [k_high, k_low, *itertools.chain(*pieces)] + ([before] if accumulate else [])
    operands = [pltpu.with_memory_space_constraint(a, pltpu.VMEM) for a in operands]
    scratch = [pltpu.VMEM((count * depth, width), HALF)] * 2
    alias = {}
    if last:
        scratch += [pltpu.VMEM((rows, width), jnp.float32), pltpu.SemaphoreType.DMA((TILES[1] * COPIES,))]
        shape = jax.ShapeDtypeStruct((1, rows, width), jnp.float32)
    else:
        shape = pltpu.VMEM((rows, width), jnp.float32)
        alias = {len(operands) - 1: 0} if accumulate else {}
    return pl.pallas_call(
        functools.partial(multiply_kernel, start, [len(of) for of in pieces], accumulate, last),
        in_specs=[VMEM] * len(operands),
        out_specs=ANY if last else VMEM,
        out_shape=shape,
        input_output_aliases=alias,
        scratch_shapes=scratch,
        cost_estimate=pl.CostEstimate(
            flops=int(weight * rows * count * depth * width), bytes_accessed=0, transcendentals=0
        ),
        compiler_params=pltpu.CompilerParams(vmem_limit_bytes=14 * 2**20),
        name="multiply_sources",
    )(*operands)


def after(value, others):
    return value if others is None else lax.optimization_barrier((value, others))[0]


def body(densities, reduced_kernel):
    levels = lax.axis_size("irrep").bit_length() - 1
    bits = lax.axis_size("row").bit_length() - 2
    mine = densities[0]
    half = mine.shape[0] // 2
    table, signs = numbers(levels, bits)
    ks = split(table, reduced_kernel[0], 2)
    early, late = mine[:half], mine[half:]
    owners = lax.axis_size("row")
    for step in range(levels):
        early, late = [lax.optimization_barrier(part) for part in (early, late)]
        partners = [partner_of(part, step, levels) for part in (early, late)]
        partners[0] = after(partners[0], tuple(ks) if step == 0 else late)
        early = fold(early, partners[0], signs[step], step, levels)
        late = fold(late, partners[1], signs[step], step, levels)
    early, late = [lax.optimization_barrier(part[None]) for part in (early, late)]
    pieces, others = [early], [*swapped(early, 1)]
    for step in range(bits - 1):
        pieces.append(after(across(early, step, bits, 0), late))
        others += swapped(pieces[-1], 1)
        early = jnp.concatenate([early, pieces[-1]])
    first = across(early, bits - 1, bits, 0)
    pieces = [*itertools.chain(*zip(pieces, others))]
    out = multiply(*ks, [pieces], 0, None, weight=12)
    out = multiply(*ks, [[late, *swapped(late, 1)]], owners, out, weight=0)
    for step in range(bits - 1):
        second = after(across(late, step, bits, 1), out)
        out = multiply(*ks, [[second, *swapped(second, 1)]], owners + (2 << step), out)
        late = jnp.concatenate([late, second])
    first = after(first, out)
    out = multiply(*ks, [[first, *swapped(first, 2)]], 1 << bits, out)
    second = after(across(late, bits - 1, bits, 1), out)
    start = owners + (1 << bits)
    out = multiply(*ks, [[second]], start, out)
    return multiply(*ks, [swapped(second, 1)], start + second.shape[0], out, True)


def solution(mesh):
    placed = (P("irrep", "row", None), P("irrep", "row", None))
    return jax.shard_map(
        body, mesh=mesh, in_specs=placed, out_specs=P("irrep", "row", None), check_vma=False
    )
```

```python
import functools
import math

import jax
import jax.numpy as jnp
from jax import lax
from jax.experimental import pallas as pl
from jax.experimental.pallas import tpu as pltpu
from jax.sharding import PartitionSpec as P

HALF = jnp.bfloat16
AXES = ("irrep", "row")
TILES = (1, 2)
WEIGHT = 6


def exchange(value, masks):
    devices = lax.axis_size("irrep") * lax.axis_size("row")
    pairs = [(at, at ^ masks[at & 1]) for at in range(devices)]
    return lax.ppermute(value, AXES, pairs)


def turns(step, count):
    return [(step + core) % count for core in range(2)]


def across(held, step, bits):
    return exchange(held, [2 << bit for bit in turns(step, bits)])


def swapped(held, parts):
    size = held.shape[0] // parts
    return [exchange(held[at : at + size], [1, 1]) for at in range(0, held.shape[0], size)]


def gather_chips(held, steps, bits, others=None):
    for step in steps:
        held = jnp.concatenate([held, after(across(held, step, bits), others)])
    return held


def numbers(levels, bits):
    me = lax.axis_index("row").astype(jnp.int32)
    octant = lax.axis_index("irrep").astype(jnp.int32)
    core = me & 1
    half = 1 << (bits - 1)
    table = []
    for group in range(2):
        for other in range(2):
            for at in range(group * half, (group + 1) * half):
                rel = [other, other]
                for step in range(bits):
                    if at >> step & 1:
                        for side, bit in enumerate(turns(step, bits)):
                            rel[side] ^= 2 << bit
                table.append(me ^ jnp.where(core ^ other == 1, rel[1], rel[0]))
    signs = []
    for step in range(levels):
        bit = turns(step, levels)
        upper = octant >> jnp.where(core == 1, bit[1], bit[0]) & 1
        signs.append((1 - 2 * upper).astype(jnp.float32))
    return lax.optimization_barrier((jnp.stack(table).astype(jnp.int32), signs))


VMEM = pl.BlockSpec(memory_space=pltpu.VMEM)
SMEM = pl.BlockSpec(memory_space=pltpu.SMEM)
ANY = pl.BlockSpec(memory_space=pl.ANY)


def fold(holding, partner, sign, step, levels):
    total = partner + sign * holding
    if step == levels - 1:
        total = total * (1.0 / math.sqrt(lax.axis_size("irrep")))
    return lax.optimization_barrier(total)


def partner_of(holding, step, levels):
    owners = lax.axis_size("row")
    return exchange(holding, [owners << bit for bit in turns(step, levels)])


def in_two(value):
    high = value.astype(HALF)
    return high, (value - high.astype(jnp.float32)).astype(HALF)


def split_kernel(owners, chunks, table_ref, k_ref, high_ref, low_ref):
    depth = k_ref.shape[1] // owners // chunks
    for chunk in range(chunks):
        for piece in range(owners):
            start = (table_ref[piece] * chunks + chunk) * depth
            high, low = in_two(k_ref[:, pl.ds(pl.multiple_of(start, depth), depth)])
            at = (chunk * owners + piece) * depth
            high_ref[:, at : at + depth] = high
            low_ref[:, at : at + depth] = low


def split(table, k, chunks):
    rows, sources = k.shape
    tile = rows // 6
    block = pl.BlockSpec((tile, sources), lambda m, table: (m, 0))
    return pl.pallas_call(
        functools.partial(split_kernel, lax.axis_size("row"), chunks),
        grid_spec=pltpu.PrefetchScalarGridSpec(
            num_scalar_prefetch=1,
            grid=(rows // tile,),
            in_specs=[block],
            out_specs=[block, block],
        ),
        out_shape=[pltpu.VMEM((rows, sources), HALF)] * 2,
        cost_estimate=pl.CostEstimate(
            flops=4 * rows * sources, bytes_accessed=4 * rows * sources, transcendentals=0
        ),
        compiler_params=pltpu.CompilerParams(vmem_limit_bytes=18 * 2**20),
        name="split_reduced_kernel",
    )(table, pltpu.with_memory_space_constraint(k, pltpu.HBM))


def multiply_kernel(start, arrays, accumulate, last, high_ref, low_ref, *refs):
    refs = list(refs)
    f_refs = [refs.pop(0) for _ in range(arrays)]
    before = refs.pop(0) if accumulate else None
    out_ref, f_high, f_low = refs[:3]
    depth = f_refs[0].shape[1]
    at = 0
    for ref in f_refs:
        for piece in range(ref.shape[0]):
            high, low = in_two(ref[piece])
            f_high[at : at + depth, :] = high
            f_low[at : at + depth, :] = low
            at += depth
    sources = slice(start * depth, start * depth + at)
    tiles = TILES[last]
    tile = high_ref.shape[0] // tiles

    def product(step):
        here = pl.ds(pl.multiple_of(step * tile, tile), tile)
        high, low = high_ref[here, sources], low_ref[here, sources]
        left = jnp.concatenate([low, high, high], axis=1)
        right = jnp.concatenate([f_high[...], f_low[...], f_high[...]], axis=0)
        total = jnp.dot(left, right, preferred_element_type=jnp.float32)
        return here, total + before[here, :] if accumulate else total

    if not last:

        @pl.loop(0, tiles)
        def _(step):
            here, total = product(step)
            out_ref[here, :] = total

    else:
        result, sems = refs[3:]

        def copy(here, step):
            return pltpu.make_async_copy(
                result.at[here, :], out_ref.at[0, here, :], sems.at[step]
            )

        @pl.loop(0, tiles)
        def _(step):
            here, total = product(step)
            result[here, :] = total
            copy(here, step).start()

        for step in range(tiles):
            copy(slice(step * tile, (step + 1) * tile), step).wait()


def multiply(k_high, k_low, pieces, start, before, last=False):
    rows = k_high.shape[0]
    count, (depth, width) = sum(a.shape[0] for a in pieces), pieces[0].shape[1:]
    accumulate = before is not None
    operands = [k_high, k_low, *pieces] + ([before] if accumulate else [])
    operands = [pltpu.with_memory_space_constraint(a, pltpu.VMEM) for a in operands]
    scratch = [pltpu.VMEM((count * depth, width), HALF)] * 2
    alias = {}
    if last:
        scratch += [pltpu.VMEM((rows, width), jnp.float32), pltpu.SemaphoreType.DMA((TILES[1],))]
        shape = jax.ShapeDtypeStruct((1, rows, width), jnp.float32)
    else:
        shape = pltpu.VMEM((rows, width), jnp.float32)
        alias = {len(operands) - 1: 0} if accumulate else {}
    return pl.pallas_call(
        functools.partial(multiply_kernel, start, len(pieces), accumulate, last),
        in_specs=[VMEM] * len(operands),
        out_specs=ANY if last else VMEM,
        out_shape=shape,
        input_output_aliases=alias,
        scratch_shapes=scratch,
        cost_estimate=pl.CostEstimate(
            flops=int(WEIGHT * rows * count * depth * width), bytes_accessed=0, transcendentals=0
        ),
        compiler_params=pltpu.CompilerParams(vmem_limit_bytes=14 * 2**20),
        name="multiply_sources",
    )(*operands)


def after(value, others):
    return value if others is None else lax.optimization_barrier((value, others))[0]


def body(densities, reduced_kernel):
    levels = lax.axis_size("irrep").bit_length() - 1
    bits = lax.axis_size("row").bit_length() - 2
    mine = densities[0]
    half = mine.shape[0] // 2
    table, signs = numbers(levels, bits)
    ks = split(table, reduced_kernel[0], 2)
    parts = [lax.optimization_barrier(mine[at * half : (at + 1) * half]) for at in range(2)]
    for step in range(levels):
        partners = [partner_of(part, step, levels) for part in parts]
        partners[0] = after(partners[0], tuple(ks) if step == 0 else parts[1])
        parts = [fold(*pair, signs[step], step, levels) for pair in zip(parts, partners)]
    last = bits - 1
    group = lax.axis_size("row") // 2
    early = gather_chips(parts[0][None], range(last), bits)
    early = after(early, parts[1])
    arrived = across(early, last, bits)
    out = multiply(*ks, [early, exchange(early, [1, 1])], 0, None)
    late = gather_chips(parts[1][None], range(last), bits, out)
    out = multiply(*ks, [late, exchange(late, [1, 1])], 2 * group, out)
    out = multiply(*ks, [arrived, *swapped(arrived, 2)], group, out)
    arrived = after(across(late, last, bits), out)
    out = multiply(*ks, [arrived], 3 * group, out)
    return multiply(*ks, [exchange(arrived, [1, 1])], 3 * group + group // 2, out, True)


def solution(mesh):
    placed = (P("irrep", "row", None), P("irrep", "row", None))
    return jax.shard_map(
        body, mesh=mesh, in_specs=placed, out_specs=P("irrep", "row", None), check_vma=False
    )
```

```python
import functools
import math

import jax
import jax.numpy as jnp
from jax import lax
from jax.experimental import pallas as pl
from jax.experimental.pallas import tpu as pltpu
from jax.sharding import PartitionSpec as P

HALF = jnp.bfloat16
AXES = ("irrep", "row")
TILES = (1, 2)
WEIGHT = 6


def exchange(value, masks):
    devices = lax.axis_size("irrep") * lax.axis_size("row")
    pairs = [(at, at ^ masks[at & 1]) for at in range(devices)]
    return lax.ppermute(value, AXES, pairs)


def turns(step, count):
    return [(step + core) % count for core in range(2)]


def across(held, step, bits):
    return exchange(held, [2 << bit for bit in turns(step, bits)])


def swapped(held, parts):
    size = held.shape[0] // parts
    return [exchange(held[at : at + size], [1, 1]) for at in range(0, held.shape[0], size)]


def gather_chips(held, steps, bits, others=None):
    for step in steps:
        held = jnp.concatenate([held, after(across(held, step, bits), others)])
    return held


def numbers(levels, bits):
    me = lax.axis_index("row").astype(jnp.int32)
    octant = lax.axis_index("irrep").astype(jnp.int32)
    core = me & 1
    half = 1 << (bits - 1)
    table = []
    for group in range(2):
        for other in range(2):
            for at in range(group * half, (group + 1) * half):
                rel = [other, other]
                for step in range(bits):
                    if at >> step & 1:
                        for side, bit in enumerate(turns(step, bits)):
                            rel[side] ^= 2 << bit
                table.append(me ^ jnp.where(core ^ other == 1, rel[1], rel[0]))
    signs = []
    for step in range(levels):
        bit = turns(step, levels)
        upper = octant >> jnp.where(core == 1, bit[1], bit[0]) & 1
        signs.append((1 - 2 * upper).astype(jnp.float32))
    return lax.optimization_barrier((jnp.stack(table).astype(jnp.int32), signs))


VMEM = pl.BlockSpec(memory_space=pltpu.VMEM)
SMEM = pl.BlockSpec(memory_space=pltpu.SMEM)
ANY = pl.BlockSpec(memory_space=pl.ANY)


def fold(holding, partner, sign, step, levels):
    total = partner + sign * holding
    if step == levels - 1:
        total = total * (1.0 / math.sqrt(lax.axis_size("irrep")))
    return lax.optimization_barrier(total)


def partner_of(holding, step, levels):
    owners = lax.axis_size("row")
    return exchange(holding, [owners << bit for bit in turns(step, levels)])


def in_two(value):
    high = value.astype(HALF)
    return high, (value - high.astype(jnp.float32)).astype(HALF)


def split_kernel(owners, chunks, table_ref, k_ref, high_ref, low_ref):
    depth = k_ref.shape[1] // owners // chunks
    for chunk in range(chunks):
        for piece in range(owners):
            start = (table_ref[piece] * chunks + chunk) * depth
            high, low = in_two(k_ref[:, pl.ds(pl.multiple_of(start, depth), depth)])
            at = (chunk * owners + piece) * depth
            high_ref[:, at : at + depth] = high
            low_ref[:, at : at + depth] = low


def split(table, k, chunks):
    rows, sources = k.shape
    tile = rows // 8
    block = pl.BlockSpec((tile, sources), lambda m, table: (m, 0))
    return pl.pallas_call(
        functools.partial(split_kernel, lax.axis_size("row"), chunks),
        grid_spec=pltpu.PrefetchScalarGridSpec(
            num_scalar_prefetch=1,
            grid=(rows // tile,),
            in_specs=[block],
            out_specs=[block, block],
        ),
        out_shape=[pltpu.VMEM((rows, sources), HALF)] * 2,
        cost_estimate=pl.CostEstimate(
            flops=4 * rows * sources, bytes_accessed=4 * rows * sources, transcendentals=0
        ),
        compiler_params=pltpu.CompilerParams(vmem_limit_bytes=18 * 2**20),
        name="split_reduced_kernel",
    )(table, pltpu.with_memory_space_constraint(k, pltpu.HBM))


def multiply_kernel(start, arrays, accumulate, last, high_ref, low_ref, *refs):
    refs = list(refs)
    f_refs = [refs.pop(0) for _ in range(arrays)]
    before = refs.pop(0) if accumulate else None
    out_ref, f_high, f_low = refs[:3]
    depth = f_refs[0].shape[1]
    at = 0
    for ref in f_refs:
        for piece in range(ref.shape[0]):
            high, low = in_two(ref[piece])
            f_high[at : at + depth, :] = high
            f_low[at : at + depth, :] = low
            at += depth
    sources = slice(start * depth, start * depth + at)
    tiles = TILES[last]
    tile = high_ref.shape[0] // tiles

    def product(step):
        here = pl.ds(pl.multiple_of(step * tile, tile), tile)
        high, low = high_ref[here, sources], low_ref[here, sources]
        left = jnp.concatenate([low, high, high], axis=1)
        right = jnp.concatenate([f_high[...], f_low[...], f_high[...]], axis=0)
        total = jnp.dot(left, right, preferred_element_type=jnp.float32)
        return here, total + before[here, :] if accumulate else total

    if not last:

        @pl.loop(0, tiles)
        def _(step):
            here, total = product(step)
            out_ref[here, :] = total

    else:
        result, sems = refs[3:]

        def copy(here, step):
            return pltpu.make_async_copy(
                result.at[here, :], out_ref.at[0, here, :], sems.at[step]
            )

        @pl.loop(0, tiles)
        def _(step):
            here, total = product(step)
            result[here, :] = total
            copy(here, step).start()

        for step in range(tiles):
            copy(slice(step * tile, (step + 1) * tile), step).wait()


def multiply(k_high, k_low, pieces, start, before, last=False):
    rows = k_high.shape[0]
    count, (depth, width) = sum(a.shape[0] for a in pieces), pieces[0].shape[1:]
    accumulate = before is not None
    operands = [k_high, k_low, *pieces] + ([before] if accumulate else [])
    operands = [pltpu.with_memory_space_constraint(a, pltpu.VMEM) for a in operands]
    scratch = [pltpu.VMEM((count * depth, width), HALF)] * 2
    alias = {}
    if last:
        scratch += [pltpu.VMEM((rows, width), jnp.float32), pltpu.SemaphoreType.DMA((TILES[1],))]
        shape = jax.ShapeDtypeStruct((1, rows, width), jnp.float32)
    else:
        shape = pltpu.VMEM((rows, width), jnp.float32)
        alias = {len(operands) - 1: 0} if accumulate else {}
    return pl.pallas_call(
        functools.partial(multiply_kernel, start, len(pieces), accumulate, last),
        in_specs=[VMEM] * len(operands),
        out_specs=ANY if last else VMEM,
        out_shape=shape,
        input_output_aliases=alias,
        scratch_shapes=scratch,
        cost_estimate=pl.CostEstimate(
            flops=int(WEIGHT * rows * count * depth * width), bytes_accessed=0, transcendentals=0
        ),
        compiler_params=pltpu.CompilerParams(vmem_limit_bytes=14 * 2**20),
        name="multiply_sources",
    )(*operands)


def after(value, others):
    return value if others is None else lax.optimization_barrier((value, others))[0]


def body(densities, reduced_kernel):
    levels = lax.axis_size("irrep").bit_length() - 1
    bits = lax.axis_size("row").bit_length() - 2
    mine = densities[0]
    half = mine.shape[0] // 2
    table, signs = numbers(levels, bits)
    ks = split(table, reduced_kernel[0], 2)
    parts = [lax.optimization_barrier(mine[at * half : (at + 1) * half]) for at in range(2)]
    for step in range(levels):
        partners = [partner_of(part, step, levels) for part in parts]
        partners[0] = after(partners[0], tuple(ks) if step == 0 else parts[1])
        parts = [fold(*pair, signs[step], step, levels) for pair in zip(parts, partners)]
    last = bits - 1
    group = lax.axis_size("row") // 2
    early = gather_chips(parts[0][None], range(last), bits)
    early = after(early, parts[1])
    arrived = across(early, last, bits)
    out = multiply(*ks, [early, exchange(early, [1, 1])], 0, None)
    late = gather_chips(parts[1][None], range(last), bits, out)
    out = multiply(*ks, [late, exchange(late, [1, 1])], 2 * group, out)
    out = multiply(*ks, [arrived, *swapped(arrived, 2)], group, out)
    arrived = after(across(late, last, bits), out)
    out = multiply(*ks, [arrived], 3 * group, out)
    return multiply(*ks, [exchange(arrived, [1, 1])], 3 * group + group // 2, out, True)


def solution(mesh):
    placed = (P("irrep", "row", None), P("irrep", "row", None))
    return jax.shard_map(
        body, mesh=mesh, in_specs=placed, out_specs=P("irrep", "row", None), check_vma=False
    )
```
